256 devices in a mesh: section: 16 (over y, z_hi), tensor: 16 (over x, z_lo, core).
Axes of the slice: x: 4, y: 4, z: 8 (z_hi: 4, z_lo: 2; z = z_hi * 2 + z_lo), core: 2. Of those that a mesh axis runs over, the one named last changes fastest.
Arguments:
- store: bfloat16 [64, 640, 2048], P('section', None, 'tensor'), as said below
- owners: int32 [16], replicated, may hold values from 0 to 63, as said below
- positions: int32 [16], replicated, may hold values from 0 to 9600, as said below
- sel_rows: int32 [16, 96], replicated, may hold values from 0 to 639, as said below
- sel_hidden: bfloat16 [16, 96, 12288], P(None, None, 'section'), as said below
- norm_gain: bfloat16 [12288], P('section'), may hold values from 0.099609375 to 1.8984375
- w_query: bfloat16 [12288, 12288], P('section', 'tensor'), may hold values from -0.0546875 to 0.0546875
- w_keyval: bfloat16 [12288, 2048], P('section', 'tensor'), may hold values from -0.0546875 to 0.0546875
- w_out: bfloat16 [12288, 12288], P('tensor', 'section'), may hold values from -0.5 to 0.5
Outputs:
- blended_cache: bfloat16 [16, 640, 2048], P('section', None, 'tensor')
- mixed: bfloat16 [16, 96, 12288], P('tensor', None, 'section')
The draws below stay inside these ranges and needn't reach their ends.
Inputs may be any that keep to these rules, and one draw needn't show every extreme that they name: `owners`: slot of each group's cache; slot s lies on section index s // 4. Groups use distinct slots, and one section index holds 4 of the groups in every draw. `positions`: 640 times a permutation of the group numbers. `sel_rows`: 96 distinct rows of each group, in increasing order. `store`: cached keys and values of each slot. `sel_hidden`: hidden states at the recomputed rows.
All inputs are finite; a program needn't handle non-finite values.
Results may differ from the reference program's by a relative error of at most 0.025.
The reference program's roundings to bfloat16 on the way count: a program that leaves them out, or rounds other values in their place, can miss the bound.
Values may be sent and summed in bfloat16 or wider, within the bound.
A program may use at most 128 MiB of HBM per device.

```python
import math
import jax
import jax.numpy as jnp
from jax import lax

D = 12288
HEADS = 96
KVH = 8
HD = 128
HALF = 6
L = 640
SEL = 96
SLOT_DEV = 4
GROUPS = 16
SLOTS = 64


def draw_store(key, part):
    key = jax.random.fold_in(key, 11)
    normal_part = jax.random.normal(key, (SLOTS, L, 2 * KVH * HD), jnp.float32)
    return normal_part.astype(jnp.bfloat16)


def draw_owners(key, part):
    key = jax.random.fold_in(key, 23)
    device_count = SLOTS // SLOT_DEV
    group_order = jax.random.permutation(jax.random.fold_in(key, 1), GROUPS).astype(jnp.int32)
    if SLOT_DEV == GROUPS:
        hot_device = jnp.asarray(device_count - 1, jnp.int32)
    else:
        hot_device = jax.random.randint(jax.random.fold_in(key, 2), (), 0, device_count).astype(jnp.int32)
    slot_order = jax.random.permutation(jax.random.fold_in(key, 3), SLOTS).astype(jnp.int32)
    on_hot = (slot_order // SLOT_DEV == hot_device).astype(jnp.int32)
    not_last = (slot_order != SLOTS - 1).astype(jnp.int32)
    sort_key = on_hot * 2 + not_last
    free_slots = slot_order[jnp.argsort(sort_key, stable=True)]
    hot_slots = hot_device * SLOT_DEV + jnp.arange(SLOT_DEV, dtype=jnp.int32)
    assigned = jnp.concatenate([hot_slots, free_slots[:GROUPS - SLOT_DEV]])
    return jnp.zeros((GROUPS,), jnp.int32).at[group_order].set(assigned)


def draw_positions(key, part):
    key = jax.random.fold_in(key, 37)
    return (jax.random.permutation(key, GROUPS).astype(jnp.int32) * L).astype(jnp.int32)


def draw_sel_rows(key, part):
    key = jax.random.fold_in(key, 53)
    row_keys = jax.random.split(key, GROUPS)

    def choose(row_key):
        return jnp.sort(jax.random.permutation(row_key, L).astype(jnp.int32)[:SEL])
    return jax.vmap(choose)(row_keys).astype(jnp.int32)


def draw_sel_hidden(key, part):
    key = jax.random.fold_in(key, 41)
    column = jnp.arange(D, dtype=jnp.float32) / (D - 1)
    normal_part = jax.random.normal(key, (GROUPS, SEL, D), jnp.float32)
    return (normal_part * (1.0 + 2.0 * column)).astype(jnp.bfloat16)


def levels(own_key, shape, pieces, smallest, top_value):
    def one(position, blocks):
        steps = jax.random.uniform(jax.random.fold_in(jax.random.fold_in(own_key, 6), position), (blocks,), jnp.float32, smallest / len(pieces), top_value / len(pieces))
        return jnp.repeat(jnp.exp(steps), shape[position] // blocks).reshape((-1,) + (1,) * (len(shape) - position - 1))

    factor_of = one(*pieces[0])
    for cut in pieces[1:]:
        factor_of = factor_of * one(*cut)
    return factor_of


def bell_draw(key, dims, scale, limit, cuts=(), kind=jnp.bfloat16):
    drawn = jax.random.normal(key, dims, jnp.float32) * scale
    if len(cuts) > 0:
        drawn = levels(key, dims, cuts, -0.22, 0.18) * drawn
    return jnp.clip(drawn, min=-limit, max=limit).astype(kind)


def setup_inputs(seed: int = 0) -> dict:
    splits = jax.random.split(jax.random.key(seed), 10)
    return {
        "store": draw_store(jax.random.fold_in(splits[9], 71), 0),
        "owners": draw_owners(jax.random.fold_in(splits[9], 71), 0),
        "positions": draw_positions(jax.random.fold_in(splits[9], 71), 0),
        "sel_rows": draw_sel_rows(jax.random.fold_in(splits[9], 71), 0),
        "sel_hidden": draw_sel_hidden(jax.random.fold_in(splits[9], 71), 0),
        "norm_gain": jnp.clip(1.0 + 0.18 * jax.random.normal(splits[5], (D,), jnp.float32), 0.099609375, 1.8984375).astype(jnp.bfloat16),
        "w_query": bell_draw(splits[6], (D, HEADS * HD), D ** -0.5, 0.0546875, ((0, 16), (1, 16))),
        "w_keyval": bell_draw(splits[7], (D, 2 * KVH * HD), D ** -0.5, 0.0546875, ((0, 16), (1, 16))),
        "w_out": bell_draw(splits[8], (HEADS * HD, D), HD ** -0.5, 0.5, ((0, 16), (1, 16))),
    }


THETA = 1000000.0
EPS = 1e-05
MASKED = -1e+30

def rotate(vectors, angle_at):
    head_size = vectors.shape[-1]
    half_count = head_size // 2
    freq_index = jnp.arange(half_count, dtype=jnp.float32)
    frequency = jnp.power(THETA, -2.0 * freq_index / head_size)
    phase_angle = angle_at[..., None] * frequency
    cosine = jnp.cos(phase_angle)
    sine_part = jnp.sin(phase_angle)
    first_half = vectors[..., :half_count]
    second_half = vectors[..., half_count:]
    return jnp.concatenate([first_half * cosine - second_half * sine_part, second_half * cosine + first_half * sine_part], -1)

def reference(store, owners, positions, sel_rows, sel_hidden, norm_gain, w_query, w_keyval, w_out):
    score_scale = 1.0 / math.sqrt(HD)
    cached = jnp.take(store, owners, axis=0).reshape(GROUPS, L, 2, KVH, HD)
    shift_pos = jnp.broadcast_to(positions.astype(jnp.float32)[:, None, None], (GROUPS, L, KVH))
    shifted = rotate(cached[:, :, 0].astype(jnp.float32), shift_pos).astype(jnp.bfloat16)
    old_values = cached[:, :, 1]
    hidden_f32 = sel_hidden.astype(jnp.float32)
    squares = lax.optimization_barrier(jnp.sum(hidden_f32 * hidden_f32, axis=-1, keepdims=True))
    normed = (hidden_f32 * lax.rsqrt(squares / D + EPS) * norm_gain.astype(jnp.float32)).astype(jnp.bfloat16)
    flat_normed = normed.reshape(GROUPS * SEL, D)
    query_raw = jnp.dot(flat_normed, w_query, preferred_element_type=jnp.float32).reshape(GROUPS, SEL, 2, KVH, HALF, HD)
    fresh_raw = jnp.dot(flat_normed, w_keyval, preferred_element_type=jnp.float32).reshape(GROUPS, SEL, 2, KVH, HD)
    query_pos = (positions[:, None] + sel_rows).astype(jnp.int32)
    query_float = query_pos.astype(jnp.float32)
    queries = rotate(query_raw, jnp.broadcast_to(query_float[:, :, None, None, None], (GROUPS, SEL, 2, KVH, HALF))).astype(jnp.bfloat16)
    fresh_keys = rotate(fresh_raw[:, :, 0], jnp.broadcast_to(query_float[:, :, None], (GROUPS, SEL, KVH))).astype(jnp.bfloat16)
    fresh_values = fresh_raw[:, :, 1].astype(jnp.bfloat16)
    group_ids = jnp.arange(GROUPS, dtype=jnp.int32)[:, None]
    blend_keys = shifted.at[group_ids, sel_rows].set(fresh_keys)
    blend_values = old_values.at[group_ids, sel_rows].set(fresh_values)
    blended_cache = jnp.stack([blend_keys, blend_values], axis=2).reshape(GROUPS, L, 2 * KVH * HD)
    all_keys = blend_keys.reshape(GROUPS * L, KVH, HD).astype(jnp.float32)
    all_values = blend_values.reshape(GROUPS * L, KVH, HD).astype(jnp.float32)
    key_pos = (positions[:, None] + jnp.arange(L, dtype=jnp.int32)[None, :]).reshape(GROUPS * L)

    def attend(inputs):
        group_queries, target_pos = inputs
        scores = jnp.einsum('sagjd,kgd->sagjk', group_queries.astype(jnp.float32), all_keys) * score_scale
        visible = (key_pos[None, :] <= target_pos[:, None])[:, None, None, None, :]
        scores = jnp.where(visible, scores, MASKED)
        top_score = lax.optimization_barrier(jnp.max(scores, axis=-1, keepdims=True))
        weights = jnp.where(visible, jnp.exp(scores - top_score), 0.0)
        weight_total = lax.optimization_barrier(jnp.sum(weights, axis=-1))
        rounded = lax.optimization_barrier(weights.astype(jnp.bfloat16)).astype(jnp.float32)
        numerator = jnp.einsum('sagjk,kgd->sagjd', rounded, all_values)
        return (numerator / weight_total[..., None]).astype(jnp.bfloat16)
    attended = lax.map(attend, (queries, query_pos))
    mixed = jnp.dot(attended.reshape(GROUPS * SEL, HEADS * HD), w_out, preferred_element_type=jnp.float32)
    mixed = mixed.astype(jnp.bfloat16).reshape(GROUPS, SEL, D)
    return (blended_cache, mixed)
```

```python
import math

import jax
import jax.numpy as jnp
from jax import lax
from jax.experimental import pallas as pl
from jax.experimental.pallas import tpu as pltpu
from jax.sharding import PartitionSpec as P

D = 12288
HD = 128
HALF = 6
L = 640
SEL = 96
THETA = 1000000.0
EPS = 1e-05
MASKED = -1e30
MESH = pl.DeviceIdType.MESH
F32 = jnp.float32
BF16 = jnp.bfloat16
QW = 768
PW = 896
QPAD = 640
SCALE2 = math.log2(math.e) / math.sqrt(HD)


def along(section=None, tensor=None):
    where = {}
    if section is not None:
        where["section"] = section
    if tensor is not None:
        where["tensor"] = tensor
    return where


def greet(peers):
    barrier = pltpu.get_barrier_semaphore()
    for peer in peers:
        pl.semaphore_signal(barrier, inc=1, device_id=peer, device_id_type=MESH)
    pl.semaphore_wait(barrier, len(peers))


def spread(vec, lanes):
    return lax.dot_general(
        vec, jnp.ones((8, lanes), F32), (((0,), (0,)), ((), ())),
        precision=lax.Precision.HIGHEST, preferred_element_type=F32,
    )


def front(owners, h, gain, wq, wkv, store, trig, rows,
          blended, kv, q,
          stbuf, stsend, strecv, p2, p2r, acc, psend, precv, zsend, zrecv,
          sqs, sqr, sqz, sqzr, fresh, ssem, rsem):
    s = lax.axis_index("section")
    t = lax.axis_index("tensor")
    y, z = s // 4, s % 4
    kind = t // 8

    def ypeer(d):
        return along(section=((y + d) % 4) * 4 + z)

    def zpeer(d):
        return along(section=y * 4 + (z + d) % 4)

    partner = along(tensor=(t + 8) % 16)
    sent = []

    def push(i, src, dst, dev):
        c = pltpu.make_async_remote_copy(
            src_ref=src, dst_ref=dst, send_sem=ssem.at[i], recv_sem=rsem.at[i],
            device_id=dev, device_id_type=MESH)
        c.start()
        sent.append(c)
        return c

    greet([ypeer(1), ypeer(2), ypeer(3), zpeer(1), zpeer(2), zpeer(3), partner])

    st_up = push(0, store, stbuf.at[y], ypeer(1))
    st_dn = push(1, store, stbuf.at[y], ypeer(3))

    ones8 = jnp.ones((8, 128), F32)

    def multiply(d, out, i):
        hf = h[pl.ds(((y + d) % 4) * 4, 4)].astype(F32).reshape(384, 768)
        hg = (hf * gain[...].astype(F32)).astype(BF16)
        a = jnp.dot(hg, wq[...], preferred_element_type=F32)
        b = jnp.dot(hg, wkv[...], preferred_element_type=F32)
        out[i, :, :, :QW] = a.reshape(4, SEL, QW).astype(out.dtype)
        out[i, :, :, QW:] = b.reshape(4, SEL, HD).astype(out.dtype)
        sq = hf * hf
        part = sq[:, :128]
        for k in range(1, 6):
            part = part + sq[:, k * 128:(k + 1) * 128]
        sqs[d] = jnp.zeros((8, 128), F32)
        for g in range(4):
            row = lax.dot_general(
                ones8, part[g * SEL:(g + 1) * SEL], (((1,), (1,)), ((), ())),
                precision=lax.Precision.HIGHEST, preferred_element_type=F32)
            sqs[d, g:g + 1, :SEL] = row[:1]

    multiply(2, p2, 0)
    up2 = push(2, p2.at[0, pl.ds(0, 2)], p2r.at[0], ypeer(1))
    dn2 = push(3, p2.at[0, pl.ds(2, 2)], p2r.at[1], ypeer(3))
    sq_y = [push(8, sqs.at[2], sqr.at[2], ypeer(2))]
    multiply(1, acc, 1)
    sq_y.append(push(9, sqs.at[1], sqr.at[3], ypeer(1)))
    multiply(3, acc, 2)
    sq_y.append(push(10, sqs.at[3], sqr.at[1], ypeer(3)))
    multiply(0, acc, 0)
    stbuf[y] = store[...]

    up2.wait_recv()
    psend[0, :2] = (acc[1, :2] + p2r[0].astype(F32)).astype(BF16)
    psend[0, 2:] = acc[1, 2:].astype(BF16)
    up1 = push(4, psend.at[0], precv.at[0], ypeer(1))
    dn2.wait_recv()
    psend[1, 2:] = (acc[2, 2:] + p2r[1].astype(F32)).astype(BF16)
    psend[1, :2] = acc[2, :2].astype(BF16)
    dn1 = push(5, psend.at[1], precv.at[1], ypeer(3))

    st_up.wait_recv()
    below = (y + 3) % 4
    above = (y + 1) % 4
    st_up2 = push(6, stbuf.at[below, pl.ds(0, 2)], stbuf.at[below, pl.ds(0, 2)], ypeer(1))
    st_dn.wait_recv()
    st_dn2 = push(7, stbuf.at[above, pl.ds(2, 2)], stbuf.at[above, pl.ds(2, 2)], ypeer(3))

    for c in sq_y:
        c.wait_recv()
    sqz[...] = sqs[0] + sqr[1] + sqr[2] + sqr[3]
    sq_z = [push(11 + d, sqz, sqzr.at[4 - d], zpeer(d)) for d in (1, 2, 3)]

    st_up2.wait_recv()
    st_dn2.wait_recv()

    def picked(d):
        slot = owners[y * 4 + (z + d) % 4]
        here = ((slot >> 2) & 3) == z
        block = stbuf[slot >> 4, slot & 3]
        return jnp.where(here, block, jnp.zeros_like(block))

    st_z = []
    for d in (2, 1, 3):
        stsend[d] = picked(d)
        st_z.append(push(15 + d, stsend.at[d], strecv.at[4 - d], zpeer(d)))

    up1.wait_recv()
    dn1.wait_recv()
    total = acc.at[0]
    pr_z = []
    for d in (2, 1, 3):
        g = (z + d) % 4
        zsend[d] = (total[g] + precv[0, g].astype(F32) + precv[1, g].astype(F32)).astype(BF16)
        pr_z.append(push(19 + d, zsend.at[d], zrecv.at[4 - d], zpeer(d)))

    for c in sq_z:
        c.wait_recv()
    squares = sqz[...] + sqzr[1] + sqzr[2] + sqzr[3]
    mine = lax.broadcasted_iota(jnp.int32, (8, 128), 0) == z
    squares = spread(jnp.where(mine, squares, 0.0), 128)[:SEL]
    inv = lax.rsqrt(squares / D + EPS)

    for c in pr_z:
        c.wait_recv()
    cos = trig[0, :SEL]
    sin = trig[1, :SEL]

    def summed(lo):
        cols = pl.ds(lo, HD)
        v = total[z, :, cols] + precv[0, z, :, cols].astype(F32)
        v = v + precv[1, z, :, cols].astype(F32)
        for d in (1, 2, 3):
            v = v + zrecv[d, :, cols].astype(F32)
        return v * inv

    def turned(v, c, sn):
        return v * c + pltpu.roll(v, 64, 1) * sn

    for j in range(HALF):
        q[0, j * SEL:(j + 1) * SEL] = turned(summed(j * HD), cos, sin).astype(BF16)
    q_y = [push(27 + d, q.at[0, pl.ds(0, 576)], q.at[4 - d, pl.ds(0, 576)], ypeer(d))
           for d in (2, 1, 3)]
    for r in range(4):
        q[r, 576:] = jnp.zeros((QPAD - 576, HD), BF16)

    values = kind == 1
    fresh[...] = jnp.zeros_like(fresh)
    fresh[:SEL] = turned(
        summed(QW), jnp.where(values, 1.0, cos), jnp.where(values, 0.0, sin)).astype(BF16)

    cached = picked(0)
    for c in st_z:
        c.wait_recv()
    for d in (1, 2, 3):
        cached = cached + strecv[d]
    shift_cos = jnp.where(values, 1.0, trig[0, SEL:SEL + 1])
    shift_sin = jnp.where(values, 0.0, trig[1, SEL:SEL + 1])
    shifted = turned(cached.astype(F32), shift_cos, shift_sin).astype(BF16)
    hit = lax.broadcasted_iota(jnp.int32, (L, 128), 0) == rows[...]
    hot = jnp.where(hit, 1.0, 0.0)
    placed = jnp.dot(hot.astype(BF16), fresh[...], preferred_element_type=F32)
    patched = jnp.where(jnp.max(hot, axis=1, keepdims=True) > 0.0, placed, shifted.astype(F32))
    patched = patched.astype(BF16)
    blended[...] = patched
    kv[kind, 0] = patched
    kv_z = [push(31 + d, kv.at[kind, 0], kv.at[kind, 4 - d], zpeer(d)) for d in (2, 1, 3)]
    kv_x = [push(35, kv.at[kind, 0], kv.at[kind, 0], partner)]
    for d, c in zip((2, 1, 3), kv_z):
        c.wait_recv()
        r = 4 - d
        kv_x.append(push(35 + r, kv.at[kind, r], kv.at[kind, r], partner))
    for c in kv_x:
        c.wait_recv()
    for c in q_y:
        c.wait_recv()
    for c in sent:
        c.wait_send()


def attend(positions, q, kv, limit, o, lse, sbuf, pbuf):
    s = lax.axis_index("section")
    y, z = s // 4, s % 4

    def tile(i, carry):
        cols = pl.ds(pl.multiple_of(i * 256, 256), 256)
        lane = i * 256 + lax.broadcasted_iota(jnp.int32, (1, 256), 1)
        first = jnp.full((1, 256), positions[y * 4 + z], jnp.int32)
        for d in (1, 2, 3):
            first = jnp.where(lane >= d * QPAD, positions[((y + d) % 4) * 4 + z], first)
        block = q[cols]
        lim = limit[:, cols]
        top = jnp.full((1, 256), MASKED, F32)
        hidden = []
        for e in range(4):
            sc = lax.dot_general(
                kv[0, e], block, (((1,), (1,)), ((), ())), preferred_element_type=F32)
            if e == 0:
                sc = jnp.where(lax.broadcasted_iota(jnp.int32, (L, 256), 0) <= lim, sc, MASKED)
            sbuf[e] = sc
            hid = positions[y * 4 + (z + e) % 4] > first
            hidden.append(hid)
            top = jnp.maximum(
                top, jnp.where(hid, MASKED, jnp.max(sc, axis=0, keepdims=True)))
        top = top * SCALE2
        weight = jnp.zeros((1, 256), F32)
        for e in range(4):
            base = top + jnp.where(hidden[e], 1e30, 0.0)
            p = jnp.exp2(sbuf[e] * SCALE2 - base)
            weight = weight + jnp.sum(p, axis=0, keepdims=True)
            pbuf[e] = p.astype(BF16)
        num = lax.dot_general(
            kv[1].reshape(4 * L, HD), pbuf[...].reshape(4 * L, 256), (((0,), (0,)), ((), ())),
            preferred_element_type=F32)
        some = weight > 0.0
        safe = jnp.where(some, weight, 1.0)
        o[cols] = (num * (1.0 / safe)).T.astype(BF16)
        lse[:, cols] = jnp.broadcast_to(
            jnp.where(some, top + jnp.log2(safe), MASKED), (8, 256))
        return carry

    lax.fori_loop(0, 4 * QPAD // 256, tile, 0)


def back(o, lse, w, out,
         orecv, lrecv, ag, prod, crecv, csum, xrecv, zlsend, zlrecv, ssem, rsem):
    s = lax.axis_index("section")
    t = lax.axis_index("tensor")
    y, z = s // 4, s % 4
    x, zl, core = t // 4, (t // 2) % 2, t % 2

    def ypeer(d):
        return along(section=((y + d) % 4) * 4 + z)

    def zpeer(d):
        return along(section=y * 4 + (z + d) % 4)

    def xpeer(d):
        return along(tensor=((x + d) % 4) * 4 + t % 4)

    twin = along(tensor=x * 4 + zl * 2 + 1 - core)
    pair = along(tensor=x * 4 + (1 - zl) * 2 + core)
    sent = []

    def make(i, src, dst, dev, r=None):
        return pltpu.make_async_remote_copy(
            src_ref=src, dst_ref=dst, send_sem=ssem.at[i],
            recv_sem=rsem.at[i if r is None else r],
            device_id=dev, device_id_type=MESH)

    def push(i, src, dst, dev):
        c = make(i, src, dst, dev)
        c.start()
        sent.append(c)
        return c

    greet([ypeer(1), ypeer(2), ypeer(3), zpeer(1), zpeer(2), zpeer(3),
           xpeer(1), xpeer(2), xpeer(3), twin, pair])

    got = []
    for d in (2, 1, 3):
        got.append(push(d, o.at[d, pl.ds(0, 576)], orecv.at[4 - d], ypeer(d)))
        got.append(push(3 + d, lse.at[:, pl.ds(d * QPAD, QPAD)], lrecv.at[4 - d], ypeer(d)))
    for c in got:
        c.wait_recv()
    logs = [lse[:1, :QPAD]] + [lrecv[d, :1] for d in (1, 2, 3)]
    top = jnp.maximum(jnp.maximum(logs[0], logs[1]), jnp.maximum(logs[2], logs[3]))
    share = [jnp.exp2(v - top) for v in logs]
    whole = share[0] + share[1] + share[2] + share[3]
    line = lax.broadcasted_iota(jnp.int32, (8, QPAD), 0) == 0
    merged = jnp.zeros((576, HD), F32)
    for d in range(4):
        part = o[0, :576] if d == 0 else orecv[d]
        col = spread(jnp.where(line, share[d] / whole, 0.0), HD)[:576]
        merged = merged + part.astype(F32) * col
    for j in range(HALF):
        ag[0, z, :, j * HD:(j + 1) * HD] = merged[j * SEL:(j + 1) * SEL].astype(BF16)

    def grp(d):
        return (z + d) % 4

    zs = {d: push(6 + d, ag.at[0, z], ag.at[0, z], zpeer(d)) for d in (2, 1, 3)}
    ups, dns = {}, {}
    for d in (0, 1, 3, 2):
        if d:
            zs[4 - d].wait_recv()
        ups[d] = push(10 + d, ag.at[0, grp(d)], ag.at[3, grp(d)], ypeer(1))
        dns[d] = push(14 + d, ag.at[0, grp(d)], ag.at[1, grp(d)], ypeer(3))

    def multiply(r):
        a = jnp.dot(ag[r].reshape(384, 768), w[...], preferred_element_type=F32)
        a = a.reshape(4, SEL, 768).astype(BF16)
        for g in range(4):
            prod[r, g % 2, g // 2] = a[g]
        return push(22 + r, prod.at[r, 1 - core], crecv.at[r], twin)

    def send_x(r, c):
        c.wait_recv()
        csum[r] = (prod[r, core].astype(F32) + crecv[r].astype(F32)).astype(BF16)
        d = (y + r + 4 - x) % 4

        @pl.when(d != 0)
        def _():
            make(26 + r, csum.at[r], xrecv.at[(4 - d) % 4], xpeer(d), 30 + (4 - d) % 4).start()

    tw0 = multiply(0)
    fw_up, fw_dn = {}, {}
    for d in (0, 1, 3, 2):
        ups[d].wait_recv()
        dns[d].wait_recv()
        if d in (0, 1):
            fw_up[d] = push(18 + d, ag.at[3, grp(d)], ag.at[2, grp(d)], ypeer(1))
        else:
            fw_dn[d] = push(18 + d, ag.at[1, grp(d)], ag.at[2, grp(d)], ypeer(3))
    send_x(0, tw0)
    tw1 = multiply(1)
    tw3 = multiply(3)
    send_x(1, tw1)
    send_x(3, tw3)
    for d in (0, 1):
        fw_up[d].wait_recv()
    for d in (3, 2):
        fw_dn[d].wait_recv()
    tw2 = multiply(2)
    send_x(2, tw2)

    for d in (1, 2, 3):
        make(26, csum.at[0], xrecv.at[d], xpeer(d), 30 + d).wait_recv()
    own = (x + 4 - y) % 4

    def reduced(k):
        v = csum[own, k].astype(F32)
        for d in (1, 2, 3):
            v = v + xrecv[d, k].astype(F32)
        return v

    zlsend[...] = reduced(1 - zl).astype(BF16)
    last = push(34, zlsend, zlrecv, pair)
    keep = reduced(zl)
    last.wait_recv()
    out[...] = (keep + zlrecv[...].astype(F32)).astype(BF16)
    for r in range(4):
        @pl.when((y + r + 4 - x) % 4 != 0)
        def _():
            make(26 + r, csum.at[r], xrecv.at[1], xpeer(1), 31).wait_send()
    for c in sent:
        c.wait_send()


VM = pl.BlockSpec(memory_space=pltpu.VMEM)
SM = pl.BlockSpec(memory_space=pltpu.SMEM)


def shards(store, owners, positions, sel_rows, sel_hidden, norm_gain, w_query, w_keyval, w_out):
    section = lax.axis_index("section")
    my_start = lax.dynamic_index_in_dim(positions, section, 0, keepdims=False)
    my_rows = lax.dynamic_index_in_dim(sel_rows, section, 0, keepdims=False)
    where = jnp.concatenate([my_start + my_rows, jnp.full((8,), my_start)]).astype(F32)
    freq_index = jnp.arange(HD // 2, dtype=F32)
    frequency = jnp.power(THETA, -2.0 * freq_index / HD)
    angle = where[:, None] * frequency
    cos, sin = jnp.cos(angle), jnp.sin(angle)
    trig = jnp.stack([jnp.concatenate([cos, cos], 1), jnp.concatenate([-sin, sin], 1)])
    rows = jnp.concatenate([my_rows, jnp.full((128 - SEL,), -1, jnp.int32)])[None]
    limit = jnp.concatenate(
        [jnp.tile(my_rows, HALF), jnp.full((4 * QPAD - 576,), L, jnp.int32)])[None]

    blended, kv, q = pl.pallas_call(
        front,
        name="front",
        out_shape=(
            jax.ShapeDtypeStruct((L, HD), BF16),
            jax.ShapeDtypeStruct((2, 4, L, HD), BF16),
            jax.ShapeDtypeStruct((4, QPAD, HD), BF16),
        ),
        in_specs=[SM] + [VM] * 7,
        out_specs=(VM, VM, VM),
        scratch_shapes=[
            pltpu.VMEM((4, 4, L, HD), BF16),
            pltpu.VMEM((4, L, HD), BF16),
            pltpu.VMEM((4, L, HD), BF16),
            pltpu.VMEM((1, 4, SEL, PW), BF16),
            pltpu.VMEM((2, 2, SEL, PW), BF16),
            pltpu.VMEM((3, 4, SEL, PW), F32),
            pltpu.VMEM((2, 4, SEL, PW), BF16),
            pltpu.VMEM((2, 4, SEL, PW), BF16),
            pltpu.VMEM((4, SEL, PW), BF16),
            pltpu.VMEM((4, SEL, PW), BF16),
            pltpu.VMEM((4, 8, 128), F32),
            pltpu.VMEM((4, 8, 128), F32),
            pltpu.VMEM((8, 128), F32),
            pltpu.VMEM((4, 8, 128), F32),
            pltpu.VMEM((128, HD), BF16),
            pltpu.SemaphoreType.DMA((39,)),
            pltpu.SemaphoreType.DMA((39,)),
        ],
        compiler_params=pltpu.CompilerParams(
            collective_id=0, has_side_effects=True, vmem_limit_bytes=56 * 2**20),
    )(owners, sel_hidden, norm_gain[None], w_query, w_keyval, store, trig, rows)

    o, lse = pl.pallas_call(
        attend,
        name="attend",
        out_shape=(
            jax.ShapeDtypeStruct((4 * QPAD, HD), BF16),
            jax.ShapeDtypeStruct((8, 4 * QPAD), F32),
        ),
        in_specs=[SM] + [VM] * 3,
        out_specs=(VM, VM),
        scratch_shapes=[
            pltpu.VMEM((4, L, 256), F32),
            pltpu.VMEM((4, L, 256), BF16),
        ],
        compiler_params=pltpu.CompilerParams(vmem_limit_bytes=56 * 2**20),
    )(positions, q.reshape(4 * QPAD, HD), kv, limit)

    mixed = pl.pallas_call(
        back,
        name="back",
        out_shape=jax.ShapeDtypeStruct((SEL, 768), BF16),
        in_specs=[VM] * 3,
        out_specs=VM,
        scratch_shapes=[
            pltpu.VMEM((4, 576, HD), BF16),
            pltpu.VMEM((4, 8, QPAD), F32),
            pltpu.VMEM((4, 4, SEL, 768), BF16),
            pltpu.VMEM((4, 2, 2, SEL, 768), BF16),
            pltpu.VMEM((4, 2, SEL, 768), BF16),
            pltpu.VMEM((4, 2, SEL, 768), BF16),
            pltpu.VMEM((4, 2, SEL, 768), BF16),
            pltpu.VMEM((SEL, 768), BF16),
            pltpu.VMEM((SEL, 768), BF16),
            pltpu.SemaphoreType.DMA((35,)),
            pltpu.SemaphoreType.DMA((35,)),
        ],
        compiler_params=pltpu.CompilerParams(
            collective_id=1, has_side_effects=True, vmem_limit_bytes=56 * 2**20),
    )(o.reshape(4, QPAD, HD), lse, w_out)
    return blended[None], mixed[None]


def solution(mesh):
    return jax.shard_map(
        shards,
        mesh=mesh,
        in_specs=(
            P("section", None, "tensor"),
            P(),
            P(),
            P(),
            P(None, None, "section"),
            P("section"),
            P("section", "tensor"),
            P("section", "tensor"),
            P("tensor", "section"),
        ),
        out_specs=(P("section", None, "tensor"), P("tensor", None, "section")),
        check_vma=False,
    )
```

```python
import math

import jax
import jax.numpy as jnp
import numpy as np
from jax import lax
from jax.experimental import pallas as pl
from jax.experimental.pallas import tpu as pltpu
from jax.sharding import PartitionSpec as P

D = 12288
HD = 128
HALF = 6
L = 640
LH = L // 2
SEL = 96
THETA = 1000000.0
EPS = 1e-05
MASKED = -1e30
MESH = pl.DeviceIdType.MESH
F32 = jnp.float32
BF16 = jnp.bfloat16
PW = 896
QN = HALF * SEL
QPAD = 640
SCALE2 = math.log2(math.e) / math.sqrt(HD)
CHUNKS = [(0, 128), (128, 256), (384, 256), (640, 256)]
SLOT = {0: 0, 1: 1, 3: 2, 2: 3}
SEMS = 140


def spread(vec, lanes):
    return lax.dot_general(
        vec, jnp.ones((8, lanes), F32), (((0,), (0,)), ((), ())),
        precision=lax.Precision.HIGHEST, preferred_element_type=F32,
    )


def turned(v, c, sn):
    return v * c + pltpu.roll(v, 64, 1) * sn


def sublayer(owners, positions, rows, gain, freq, h_any, wq_any, wkv_any, store, wo_any,
             blended, mixed,
             h, wq, wkv, wo, st0, st1, stsend, strecv, p2, p2r, acc, psend, precv, zsend, zrecv,
             sqs, sqr, sqz, sqzr, trig, kvc, fr, keys, vt, first_kv, q, sbuf, pbuf, o, lse,
             orecv, lrecv, ag, prod, crecv, csum, xrecv, zlsend, zlrecv, ssem, rsem, lsem):
    s = lax.axis_index("section")
    t = lax.axis_index("tensor")
    y, z = s // 4, s % 4
    x, zl, core = t // 4, (t // 2) % 2, t % 2
    kind = t // 8
    values = kind == 1

    def ypeer(d):
        return {"section": ((y + d) % 4) * 4 + z}

    def zpeer(d):
        return {"section": y * 4 + (z + d) % 4}

    def xpeer(d):
        return {"tensor": ((x + d) % 4) * 4 + t % 4}

    twin = {"tensor": x * 4 + zl * 2 + 1 - core}
    pair = {"tensor": x * 4 + (1 - zl) * 2 + core}
    partner = xpeer(2)
    sent = []
    ids = [0]

    def push(src, dst, dev):
        i = ids[0]
        ids[0] += 1
        c = pltpu.make_async_remote_copy(
            src_ref=src, dst_ref=dst, send_sem=ssem.at[i], recv_sem=rsem.at[i],
            device_id=dev, device_id_type=MESH)
        c.start()
        sent.append(c)
        return c

    def waits(copies):
        for c in copies:
            c.wait_recv()

    st = [st0, st1]
    local = []

    def fetch(src, dst):
        c = pltpu.make_async_copy(src, dst, lsem.at[len(local)])
        c.start()
        local.append(c)

    fetch(h_any, h)
    fetch(wq_any, wq)
    fetch(wkv_any, wkv)
    fetch(store.at[:, pl.ds(0, LH)], st0.at[y])
    fetch(store.at[:, pl.ds(LH, LH)], st1.at[y])
    fetch(wo_any, wo)

    peers = [f(d) for f in (ypeer, zpeer, xpeer) for d in (1, 2, 3)] + [twin, pair]
    barrier = pltpu.get_barrier_semaphore()
    for peer in peers:
        pl.semaphore_signal(barrier, inc=1, device_id=peer, device_id_type=MESH)
    pl.semaphore_wait(barrier, len(peers))

    def send_store(k):
        src = store.at[:, pl.ds(k * LH, LH)]
        return [push(src, st[k].at[y], ypeer(1)), push(src, st[k].at[y], ypeer(3))]

    def forward_store(k, copies):
        waits(copies)
        below, above = (y + 3) % 4, (y + 1) % 4
        a, b = st[k].at[below, pl.ds(0, 2)], st[k].at[above, pl.ds(2, 2)]
        return [push(a, a, ypeer(1)), push(b, b, ypeer(3))]

    def picked(k, d):
        slot = owners[y * 4 + (z + d) % 4]
        here = ((slot >> 2) & 3) == z
        block = st[k][slot >> 4, slot & 3]
        return jnp.where(here, block, jnp.zeros_like(block))

    def route_store(k, copies):
        waits(copies)
        out = []
        for d in (1, 3, 2):
            stsend[k, d] = picked(k, d)
            out.append(push(stsend.at[k, d], strecv.at[k, 4 - d], zpeer(d)))
        return out

    ones8 = jnp.ones((8, 128), F32)
    gains = gain[...].astype(F32).reshape(1, 768)

    def multiply(d, out, i):
        hf = h[pl.ds(((y + d) % 4) * 4, 4)].astype(F32).reshape(4 * SEL, 768)
        hg = (hf * gains).astype(BF16)
        a = jnp.dot(hg, wkv[...], preferred_element_type=F32)
        b = jnp.dot(hg, wq[...], preferred_element_type=F32)
        out[i, :, :, :HD] = a.reshape(4, SEL, HD).astype(out.dtype)
        out[i, :, :, HD:] = b.reshape(4, SEL, 768).astype(out.dtype)
        sq = hf * hf
        part = sq[:, :128]
        for k in range(1, 6):
            part = part + sq[:, k * 128:(k + 1) * 128]
        sqs[d] = jnp.zeros((8, 128), F32)
        for g in range(4):
            row = lax.dot_general(
                ones8, part[g * SEL:(g + 1) * SEL], (((1,), (1,)), ((), ())),
                precision=lax.Precision.HIGHEST, preferred_element_type=F32)
            sqs[d, g:g + 1, :SEL] = row[:1]

    st_a = send_store(0)
    for c in local[:3]:
        c.wait()
    multiply(2, p2, 0)
    sq_y = [push(sqs.at[2], sqr.at[2], ypeer(2))]
    fw_a = forward_store(0, st_a)
    st_b = send_store(1)
    up2, dn2 = [], []
    for lo, n in CHUNKS:
        cols = pl.ds(lo, n)
        up2.append(push(p2.at[0, pl.ds(0, 2), :, cols], p2r.at[0, :, :, cols], ypeer(1)))
        dn2.append(push(p2.at[0, pl.ds(2, 2), :, cols], p2r.at[1, :, :, cols], ypeer(3)))
    multiply(1, acc, 1)
    sq_y.append(push(sqs.at[1], sqr.at[3], ypeer(1)))
    multiply(3, acc, 2)
    sq_y.append(push(sqs.at[3], sqr.at[1], ypeer(3)))
    local[3].wait()
    rt_a = route_store(0, fw_a)
    multiply(0, acc, 0)

    row8 = lax.broadcasted_iota(jnp.int32, (8, SEL), 0) == 0
    start = positions[s].astype(F32)
    my_rows = rows[pl.ds(s, 1), :].astype(F32)
    angle = spread(jnp.where(row8, my_rows + start, 0.0), HD) * freq[...]
    lane_sign = jnp.where(lax.broadcasted_iota(jnp.int32, (1, HD), 1) < 64, -1.0, 1.0)
    trig[0, :SEL] = jnp.cos(angle)
    trig[1, :SEL] = jnp.sin(angle) * lane_sign
    shift = jnp.broadcast_to(freq[...] * start, (8, HD))
    trig[0, SEL:] = jnp.where(values, 1.0, jnp.cos(shift))
    trig[1, SEL:] = jnp.where(values, 0.0, jnp.sin(shift) * lane_sign)
    q[:, QN:] = jnp.zeros((4, QPAD - QN, HD), BF16)
    tiled = (lax.broadcasted_iota(jnp.int32, (SEL, QPAD), 1) % SEL
             == lax.broadcasted_iota(jnp.int32, (SEL, QPAD), 0))
    limit = lax.dot_general(
        jnp.where(row8, my_rows, 0.0), jnp.where(tiled, 1.0, 0.0), (((1,), (0,)), ((), ())),
        precision=lax.Precision.HIGHEST, preferred_element_type=F32)[:1]

    fw_b = forward_store(1, st_b)
    up1, dn1 = [], []

    def send_near(k):
        lo, n = CHUNKS[k]
        cols = pl.ds(lo, n)
        up2[k].wait_recv()
        psend[0, :2, :, cols] = (acc[1, :2, :, cols] + p2r[0, :, :, cols].astype(F32)).astype(BF16)
        psend[0, 2:, :, cols] = acc[1, 2:, :, cols].astype(BF16)
        up1.append(push(psend.at[0, :, :, cols], precv.at[0, :, :, cols], ypeer(1)))
        dn2[k].wait_recv()
        psend[1, 2:, :, cols] = (acc[2, 2:, :, cols] + p2r[1, :, :, cols].astype(F32)).astype(BF16)
        psend[1, :2, :, cols] = acc[2, :2, :, cols].astype(BF16)
        dn1.append(push(psend.at[1, :, :, cols], precv.at[1, :, :, cols], ypeer(3)))

    send_near(0)
    waits(sq_y)
    sqz[...] = sqs[0] + sqr[1] + sqr[2] + sqr[3]
    sq_z = [push(sqz, sqzr.at[4 - d], zpeer(d)) for d in (1, 3, 2)]
    send_near(1)

    def settle(k, copies):
        cached = picked(k, 0)
        waits(copies)
        for d in (1, 2, 3):
            cached = cached + strecv[k, d]
        part = pl.ds(k * LH, LH)
        kvc[kind, 0, part] = turned(
            cached.astype(F32), trig[0, SEL:SEL + 1], trig[1, SEL:SEL + 1]).astype(BF16)
        mine = kvc.at[kind, 0, part]
        out = {4 - d: push(mine, kvc.at[kind, 4 - d, part], zpeer(d)) for d in (1, 3, 2)}
        return out, [push(mine, mine, partner)]

    kz_a, kx_a = settle(0, rt_a)
    local[4].wait()
    rt_b = route_store(1, fw_b)
    send_near(2)
    send_near(3)

    total = acc.at[0]
    pz = []

    def send_z(k):
        lo, n = CHUNKS[k]
        cols = pl.ds(lo, n)
        up1[k].wait_recv()
        dn1[k].wait_recv()
        out = []
        for d in (1, 3, 2):
            g = (z + d) % 4
            zsend[d, :, cols] = (total[g, :, cols] + precv[0, g, :, cols].astype(F32)
                                 + precv[1, g, :, cols].astype(F32)).astype(BF16)
            out.append(push(zsend.at[d, :, cols], zrecv.at[4 - d, :, cols], zpeer(d)))
        pz.append(out)

    def hand_over(k, kz, kx):
        part = pl.ds(k * LH, LH)
        for r in (3, 1, 2):
            kz[r].wait_recv()
            kx.append(push(kvc.at[kind, r, part], kvc.at[kind, r, part], partner))

    kz_b, kx_b = settle(1, rt_b)
    send_z(0)
    hand_over(0, kz_a, kx_a)
    send_z(1)

    waits(sq_z)
    squares = sqz[...] + sqzr[1] + sqzr[2] + sqzr[3]
    own = lax.broadcasted_iota(jnp.int32, (8, 128), 0) == z
    inv = lax.rsqrt(spread(jnp.where(own, squares, 0.0), HD)[:SEL] / D + EPS)

    def summed(lo):
        cols = pl.ds(lo, HD)
        v = (total[z, :, cols] + precv[0, z, :, cols].astype(F32)
             + precv[1, z, :, cols].astype(F32))
        for d in (1, 2, 3):
            v = v + zrecv[d, :, cols].astype(F32)
        return v * inv

    waits(pz[0])
    fr[kind, 0, :SEL] = turned(
        summed(0), jnp.where(values, 1.0, trig[0, :SEL]),
        jnp.where(values, 0.0, trig[1, :SEL])).astype(BF16)
    top_rows = pl.ds(0, SEL)
    fz = {4 - d: push(fr.at[kind, 0, top_rows], fr.at[kind, 4 - d, top_rows], zpeer(d))
          for d in (1, 3, 2)}
    fx = [push(fr.at[kind, 0, top_rows], fr.at[kind, 0, top_rows], partner)]
    send_z(2)
    hand_over(1, kz_b, kx_b)
    send_z(3)
    qy = {1: [], 2: [], 3: []}
    for k in (1, 2, 3):
        waits(pz[k])
        for j in (2 * k - 2, 2 * k - 1):
            q[0, j * SEL:(j + 1) * SEL] = turned(
                summed(HD + j * HD), trig[0, :SEL], trig[1, :SEL]).astype(BF16)
        part = pl.ds((k - 1) * 2 * SEL, 2 * SEL)
        for d in (1, 3, 2):
            qy[d].append(push(q.at[0, part], q.at[SLOT[4 - d], part], ypeer(d)))
        if k == 1:
            for r in (3, 1, 2):
                fz[r].wait_recv()
                fx.append(push(fr.at[kind, r, top_rows], fr.at[kind, r, top_rows], partner))

    waits(kx_a)
    waits(kx_b)
    waits(fx)
    for r in range(4):
        group = rows[pl.ds(y * 4 + (z + r) % 4, 1), :]
        hit = lax.broadcasted_iota(jnp.int32, (L, SEL), 0) == group
        hot = jnp.where(hit, 1.0, 0.0)
        taken = jnp.max(hot, axis=1, keepdims=True) > 0.0
        hot = hot.astype(BF16)
        for k in (0, 1):
            placed = jnp.dot(hot, fr[k, r, :SEL], preferred_element_type=F32)
            patched = jnp.where(taken, placed, kvc[k, r].astype(F32))
            if r == 0:
                first_kv[k] = patched.astype(BF16)
            if k == 0:
                keys[r] = patched.astype(BF16)
            else:
                vt[:, r * L:(r + 1) * L] = patched.T.astype(BF16)
    blended[...] = first_kv[kind]

    def attend(i, da, db):
        lane = lax.broadcasted_iota(jnp.int32, (1, 2 * QPAD), 1)
        at = jnp.where(lane < QPAD, positions[((y + da) % 4) * 4 + z],
                       positions[((y + db) % 4) * 4 + z])
        block = q[2 * i:2 * i + 2].reshape(2 * QPAD, HD)
        top = jnp.full((1, 2 * QPAD), MASKED, F32)
        hidden = []
        for e in range(4):
            sc = lax.dot_general(
                keys[e], block, (((1,), (1,)), ((), ())), preferred_element_type=F32)
            if i == 0 and e == 0:
                line = lax.broadcasted_iota(jnp.int32, (L, QPAD), 0).astype(F32)
                sc = jnp.concatenate(
                    [jnp.where(line <= limit, sc[:, :QPAD], MASKED), sc[:, QPAD:]], axis=1)
            sbuf[e] = sc
            hid = positions[y * 4 + (z + e) % 4] > at
            hidden.append(hid)
            top = jnp.maximum(top, jnp.where(hid, MASKED, jnp.max(sc, axis=0, keepdims=True)))
        top = top * SCALE2
        weight = jnp.zeros((1, 2 * QPAD), F32)
        for e in range(4):
            base = top + jnp.where(hidden[e], 1e30, 0.0)
            p = jnp.exp2(sbuf[e] * SCALE2 - base)
            weight = weight + jnp.sum(p, axis=0, keepdims=True)
            pbuf[e] = p.astype(BF16)
        num = jnp.dot(vt[...], pbuf[...].reshape(4 * L, 2 * QPAD), preferred_element_type=F32)
        some = weight > 0.0
        safe = jnp.where(some, weight, 1.0)
        o[2 * i:2 * i + 2] = (num * (1.0 / safe)).T.astype(BF16).reshape(2, QPAD, HD)
        logs = jnp.broadcast_to(jnp.where(some, top + jnp.log2(safe), MASKED), (8, 2 * QPAD))
        lse[2 * i] = logs[:, :QPAD]
        lse[2 * i + 1] = logs[:, QPAD:]

    got = {}

    def send_part(d):
        got[4 - d] = [push(o.at[SLOT[d], pl.ds(0, QN)], orecv.at[4 - d], ypeer(d)),
                      push(lse.at[SLOT[d]], lrecv.at[4 - d], ypeer(d))]

    waits(qy[3])
    attend(0, 0, 1)
    send_part(1)
    waits(qy[1])
    waits(qy[2])
    attend(1, 3, 2)
    send_part(2)
    send_part(3)

    for r in (3, 2, 1):
        waits(got[r])
    logs = [lse[0, :1]] + [lrecv[r, :1] for r in (1, 2, 3)]
    top = jnp.maximum(jnp.maximum(logs[0], logs[1]), jnp.maximum(logs[2], logs[3]))
    share = [jnp.exp2(v - top) for v in logs]
    whole = share[0] + share[1] + share[2] + share[3]
    line = lax.broadcasted_iota(jnp.int32, (8, QPAD), 0) == 0
    merged = jnp.zeros((QN, HD), F32)
    for r in range(4):
        part = o[0, :QN] if r == 0 else orecv[r]
        col = spread(jnp.where(line, share[r] / whole, 0.0), HD)[:QN]
        merged = merged + part.astype(F32) * col
    for j in range(HALF):
        ag[0, z, :, j * HD:(j + 1) * HD] = merged[j * SEL:(j + 1) * SEL].astype(BF16)

    def grp(d):
        return (z + d) % 4

    ups, dns = {}, {}

    def send_y(d):
        ups[d] = push(ag.at[0, grp(d)], ag.at[3, grp(d)], ypeer(1))
        dns[d] = push(ag.at[0, grp(d)], ag.at[1, grp(d)], ypeer(3))

    zs = {d: push(ag.at[0, z], ag.at[0, z], zpeer(d)) for d in (1, 3)}
    send_y(0)
    zs[2] = push(ag.at[0, z], ag.at[0, z], zpeer(2))
    for d in (3, 1, 2):
        zs[4 - d].wait_recv()
        send_y(d)
    local[5].wait()

    def multiply_out(r):
        a = jnp.dot(ag[r].reshape(4 * SEL, 768), wo[...], preferred_element_type=F32)
        a = a.reshape(4, SEL, 768).astype(BF16)
        for g in range(4):
            prod[r, g % 2, g // 2] = a[g]
        return push(prod.at[r, 1 - core], crecv.at[r], twin)

    xbase = 130

    def x_copy(r, slot):
        return pltpu.make_async_remote_copy(
            src_ref=csum.at[r], dst_ref=xrecv.at[slot], send_sem=ssem.at[xbase + r],
            recv_sem=rsem.at[xbase + slot], device_id=xpeer(4 - slot), device_id_type=MESH)

    def away(r):
        return (y + r + 4 - x) % 4

    def send_x(r, c):
        c.wait_recv()
        csum[r] = (prod[r, core].astype(F32) + crecv[r].astype(F32)).astype(BF16)

        @pl.when(away(r) != 0)
        def _():
            x_copy(r, (4 - away(r)) % 4).start()

    tw0 = multiply_out(0)
    fw = {}
    for d in (0, 3, 1, 2):
        ups[d].wait_recv()
        dns[d].wait_recv()
        if d in (0, 3):
            fw[d] = push(ag.at[3, grp(d)], ag.at[2, grp(d)], ypeer(1))
        else:
            fw[d] = push(ag.at[1, grp(d)], ag.at[2, grp(d)], ypeer(3))
    send_x(0, tw0)
    tw1 = multiply_out(1)
    tw3 = multiply_out(3)
    send_x(1, tw1)
    send_x(3, tw3)
    for d in (0, 3, 1, 2):
        fw[d].wait_recv()
    tw2 = multiply_out(2)
    send_x(2, tw2)

    for slot in (1, 2, 3):
        x_copy(0, slot).wait_recv()
    home = (x + 4 - y) % 4

    def reduced(k):
        v = csum[home, k].astype(F32)
        for slot in (1, 2, 3):
            v = v + xrecv[slot, k].astype(F32)
        return v

    zlsend[...] = reduced(1 - zl).astype(BF16)
    last = push(zlsend, zlrecv, pair)
    keep = reduced(zl)
    last.wait_recv()
    mixed[...] = (keep + zlrecv[...].astype(F32)).astype(BF16)
    for r in range(4):
        @pl.when(away(r) != 0)
        def _():
            x_copy(r, 1).wait_send()
    for c in sent:
        c.wait_send()
    assert ids[0] <= xbase


VM = pl.BlockSpec(memory_space=pltpu.VMEM)
SM = pl.BlockSpec(memory_space=pltpu.SMEM)
ANY = pl.BlockSpec(memory_space=pl.ANY)
FREQ = (THETA ** (-2.0 * (np.arange(HD) % (HD // 2)) / HD)).astype(np.float32)[None]


def shards(store, owners, positions, sel_rows, sel_hidden, norm_gain, w_query, w_keyval, w_out):
    blended, mixed = pl.pallas_call(
        sublayer,
        name="sublayer",
        out_shape=(
            jax.ShapeDtypeStruct((L, HD), BF16),
            jax.ShapeDtypeStruct((SEL, 768), BF16),
        ),
        in_specs=[SM, SM, VM, VM, VM, ANY, ANY, ANY, ANY, ANY],
        out_specs=(VM, VM),
        scratch_shapes=[
            pltpu.VMEM((16, SEL, 768), BF16),
            pltpu.VMEM((768, 768), BF16),
            pltpu.VMEM((768, HD), BF16),
            pltpu.VMEM((768, 768), BF16),
            pltpu.VMEM((4, 4, LH, HD), BF16),
            pltpu.VMEM((4, 4, LH, HD), BF16),
            pltpu.VMEM((2, 4, LH, HD), BF16),
            pltpu.VMEM((2, 4, LH, HD), BF16),
            pltpu.VMEM((1, 4, SEL, PW), BF16),
            pltpu.VMEM((2, 2, SEL, PW), BF16),
            pltpu.VMEM((3, 4, SEL, PW), F32),
            pltpu.VMEM((2, 4, SEL, PW), BF16),
            pltpu.VMEM((2, 4, SEL, PW), BF16),
            pltpu.VMEM((4, SEL, PW), BF16),
            pltpu.VMEM((4, SEL, PW), BF16),
            pltpu.VMEM((4, 8, 128), F32),
            pltpu.VMEM((4, 8, 128), F32),
            pltpu.VMEM((8, 128), F32),
            pltpu.VMEM((4, 8, 128), F32),
            pltpu.VMEM((2, SEL + 8, HD), F32),
            pltpu.VMEM((2, 4, L, HD), BF16),
            pltpu.VMEM((2, 4, SEL, HD), BF16),
            pltpu.VMEM((4, L, HD), BF16),
            pltpu.VMEM((HD, 4 * L), BF16),
            pltpu.VMEM((2, L, HD), BF16),
            pltpu.VMEM((4, QPAD, HD), BF16),
            pltpu.VMEM((4, L, 2 * QPAD), F32),
            pltpu.VMEM((4, L, 2 * QPAD), BF16),
            pltpu.VMEM((4, QPAD, HD), BF16),
            pltpu.VMEM((4, 8, QPAD), F32),
            pltpu.VMEM((4, QN, HD), BF16),
            pltpu.VMEM((4, 8, QPAD), F32),
            pltpu.VMEM((4, 4, SEL, 768), BF16),
            pltpu.VMEM((4, 2, 2, SEL, 768), BF16),
            pltpu.VMEM((4, 2, SEL, 768), BF16),
            pltpu.VMEM((4, 2, SEL, 768), BF16),
            pltpu.VMEM((4, 2, SEL, 768), BF16),
            pltpu.VMEM((SEL, 768), BF16),
            pltpu.VMEM((SEL, 768), BF16),
            pltpu.SemaphoreType.DMA((SEMS,)),
            pltpu.SemaphoreType.DMA((SEMS,)),
            pltpu.SemaphoreType.DMA((6,)),
        ],
        compiler_params=pltpu.CompilerParams(
            collective_id=0, has_side_effects=True, vmem_limit_bytes=60 * 2**20),
    )(owners, positions, sel_rows, norm_gain, jnp.asarray(FREQ),
      sel_hidden, w_query, w_keyval, store, w_out)
    return blended[None], mixed[None]


def solution(mesh):
    return jax.shard_map(
        shards,
        mesh=mesh,
        in_specs=(
            P("section", None, "tensor"),
            P(),
            P(),
            P(),
            P(None, None, "section"),
            P("section"),
            P("section", "tensor"),
            P("section", "tensor"),
            P("tensor", "section"),
        ),
        out_specs=(P("section", None, "tensor"), P("tensor", None, "section")),
        check_vma=False,
    )
```

```python
import math

import jax
import jax.numpy as jnp
import numpy as np
from jax import lax
from jax.experimental import pallas as pl
from jax.experimental.pallas import tpu as pltpu
from jax.sharding import PartitionSpec as P

D = 12288
HD = 128
HALF = 6
L = 640
SEL = 96
THETA = 1000000.0
EPS = 1e-05
MASKED = -1e30
MESH = pl.DeviceIdType.MESH
F32 = jnp.float32
BF16 = jnp.bfloat16
PW = 896
QN = HALF * SEL
QC = 2 * SEL
TQ = 4 * QC
PARTS = [(0, 128), (128, 256), (384, 256)]
NP = len(PARTS)
OC = 384
SCALE2 = math.log2(math.e) / math.sqrt(HD)
CHUNKS = [(0, 128), (128, 256), (384, 256), (640, 256)]
XBASE = 180
SEMS = 200


def spread(vec, lanes):
    return lax.dot_general(
        vec, jnp.ones((8, lanes), F32), (((0,), (0,)), ((), ())),
        precision=lax.Precision.HIGHEST, preferred_element_type=F32,
    )


def turned(v, c, sn):
    return v * c + pltpu.roll(v, 64, 1) * sn


def sublayer(owners, positions, rows, gain, freq, h_any, wq_any, wkv_any, store, wo_any,
             blended, mixed,
             h, wq, wkv, wo, st0, st1, st2, stsend, strecv, p2, p2r, acc, psend, precv, zsend,
             zrecv, sqs, sqr, sqz, sqzr, trig, kvc, fr, keys, vt, first_kv, q, sbuf, pbuf, o, lse,
             orecv, lrecv, ag, prod, crecv, csum, zlrecv, xsum, xrecv, ssem, rsem, lsem):
    s = lax.axis_index("section")
    t = lax.axis_index("tensor")
    y, z = s // 4, s % 4
    x, zl, core = t // 4, (t // 2) % 2, t % 2
    kind = t // 8
    values = kind == 1

    def ypeer(d):
        return {"section": ((y + d) % 4) * 4 + z}

    def zpeer(d):
        return {"section": y * 4 + (z + d) % 4}

    def xpeer(d):
        return {"tensor": ((x + d) % 4) * 4 + t % 4}

    twin = {"tensor": x * 4 + zl * 2 + 1 - core}
    pair = {"tensor": x * 4 + (1 - zl) * 2 + core}
    partner = xpeer(2)
    sent = []
    ids = [0]

    def push(src, dst, dev):
        i = ids[0]
        ids[0] += 1
        c = pltpu.make_async_remote_copy(
            src_ref=src, dst_ref=dst, send_sem=ssem.at[i], recv_sem=rsem.at[i],
            device_id=dev, device_id_type=MESH)
        c.start()
        sent.append(c)
        return c

    def waits(copies):
        for c in copies:
            c.wait_recv()

    st = [st0, st1, st2]
    local = []

    def fetch(src, dst):
        c = pltpu.make_async_copy(src, dst, lsem.at[len(local)])
        c.start()
        local.append(c)

    fetch(h_any, h)
    fetch(wq_any, wq)
    fetch(wkv_any, wkv)
    for k, (lo, n) in enumerate(PARTS):
        fetch(store.at[:, pl.ds(lo, n)], st[k].at[y])
    fetch(wo_any, wo)

    peers = [f(d) for f in (ypeer, zpeer, xpeer) for d in (1, 2, 3)] + [twin, pair]
    barrier = pltpu.get_barrier_semaphore()
    for peer in peers:
        pl.semaphore_signal(barrier, inc=1, device_id=peer, device_id_type=MESH)
    pl.semaphore_wait(barrier, len(peers))

    def send_store(k):
        src = store.at[:, pl.ds(*PARTS[k])]
        return [push(src, st[k].at[y], ypeer(1)), push(src, st[k].at[y], ypeer(3))]

    def forward_store(k, copies):
        waits(copies)
        below, above = (y + 3) % 4, (y + 1) % 4
        a, b = st[k].at[below, pl.ds(0, 2)], st[k].at[above, pl.ds(2, 2)]
        return [push(a, a, ypeer(1)), push(b, b, ypeer(3))]

    def picked(k, d):
        slot = owners[y * 4 + (z + d) % 4]
        here = ((slot >> 2) & 3) == z
        block = st[k][slot >> 4, slot & 3]
        return jnp.where(here, block, jnp.zeros_like(block))

    def route_store(k, copies):
        local[3 + k].wait()
        waits(copies)
        part = pl.ds(*PARTS[k])
        out = []
        for d in (1, 3, 2):
            stsend[d, part] = picked(k, d)
            out.append(push(stsend.at[d, part], strecv.at[4 - d, part], zpeer(d)))
        return out

    ones8 = jnp.ones((8, 128), F32)
    gains = gain[...].astype(F32).reshape(1, 768)

    def multiply(d, out, i):
        hf = h[pl.ds(((y + d) % 4) * 4, 4)].astype(F32).reshape(4 * SEL, 768)
        hg = (hf * gains).astype(BF16)
        a = jnp.dot(hg, wkv[...], preferred_element_type=F32)
        b = jnp.dot(hg, wq[...], preferred_element_type=F32)
        out[i, :, :, :HD] = a.reshape(4, SEL, HD).astype(out.dtype)
        out[i, :, :, HD:] = b.reshape(4, SEL, 768).astype(out.dtype)
        sq = hf * hf
        part = sq[:, :128]
        for k in range(1, 6):
            part = part + sq[:, k * 128:(k + 1) * 128]
        sqs[d] = jnp.zeros((8, 128), F32)
        for g in range(4):
            row = lax.dot_general(
                ones8, part[g * SEL:(g + 1) * SEL], (((1,), (1,)), ((), ())),
                precision=lax.Precision.HIGHEST, preferred_element_type=F32)
            sqs[d, g:g + 1, :SEL] = row[:1]

    up2, dn2, up1, dn1 = [], [], [], []

    def send_far(k):
        cols = pl.ds(*CHUNKS[k])
        up2.append(push(p2.at[0, pl.ds(0, 2), :, cols], p2r.at[0, :, :, cols], ypeer(1)))
        dn2.append(push(p2.at[0, pl.ds(2, 2), :, cols], p2r.at[1, :, :, cols], ypeer(3)))

    def send_near(k):
        cols = pl.ds(*CHUNKS[k])
        up2[k].wait_recv()
        psend[0, :2, :, cols] = (acc[1, :2, :, cols] + p2r[0, :, :, cols].astype(F32)).astype(BF16)
        psend[0, 2:, :, cols] = acc[1, 2:, :, cols].astype(BF16)
        up1.append(push(psend.at[0, :, :, cols], precv.at[0, :, :, cols], ypeer(1)))
        dn2[k].wait_recv()
        psend[1, 2:, :, cols] = (acc[2, 2:, :, cols] + p2r[1, :, :, cols].astype(F32)).astype(BF16)
        psend[1, :2, :, cols] = acc[2, :2, :, cols].astype(BF16)
        dn1.append(push(psend.at[1, :, :, cols], precv.at[1, :, :, cols], ypeer(3)))

    total = acc.at[0]

    def send_z(k):
        cols = pl.ds(*CHUNKS[k])
        up1[k].wait_recv()
        dn1[k].wait_recv()
        out = []
        for d in (1, 3, 2):
            g = (z + d) % 4
            zsend[d, :, cols] = (total[g, :, cols] + precv[0, g, :, cols].astype(F32)
                                 + precv[1, g, :, cols].astype(F32)).astype(BF16)
            out.append(push(zsend.at[d, :, cols], zrecv.at[4 - d, :, cols], zpeer(d)))
        return out

    def settle(k, copies):
        cached = picked(k, 0)
        waits(copies)
        part = pl.ds(*PARTS[k])
        for d in (1, 2, 3):
            cached = cached + strecv[d, part]
        kvc[kind, 0, part] = turned(
            cached.astype(F32), trig[0, SEL:SEL + 1], trig[1, SEL:SEL + 1]).astype(BF16)
        mine = kvc.at[kind, 0, part]
        out = {4 - d: push(mine, kvc.at[kind, 4 - d, part], zpeer(d)) for d in (1, 3)}
        return out, [push(mine, mine, partner)]

    def pass_on(k, kz, kx):
        lo, n = PARTS[k]
        part = pl.ds(lo, n)
        for r, half, to in ((1, lo, 3), (3, lo + n // 2, 1)):
            kz[r].wait_recv()
            half = pl.ds(half, n // 2)
            kz[r + 4] = push(kvc.at[kind, r, half], kvc.at[kind, 2, half], zpeer(to))
            kx.append(push(kvc.at[kind, r, part], kvc.at[kind, r, part], partner))

    def pass_far(k, kz, kx):
        part = pl.ds(*PARTS[k])
        kz[5].wait_recv()
        kz[7].wait_recv()
        kx.append(push(kvc.at[kind, 2, part], kvc.at[kind, 2, part], partner))

    sa = send_store(0)
    for c in local[:3]:
        c.wait()
    multiply(2, p2, 0)
    sb = send_store(1)
    sq_y = [push(sqs.at[2], sqr.at[2], ypeer(2))]
    fa = forward_store(0, sa)
    send_far(0)
    send_far(1)
    multiply(1, acc, 1)
    sq_y.append(push(sqs.at[1], sqr.at[3], ypeer(1)))
    ra = route_store(0, fa)
    multiply(3, acc, 2)
    sq_y.append(push(sqs.at[3], sqr.at[1], ypeer(3)))
    sc = send_store(2)
    fb = forward_store(1, sb)

    row8 = lax.broadcasted_iota(jnp.int32, (8, SEL), 0) == 0
    start = positions[s].astype(F32)
    my_rows = rows[pl.ds(s, 1), :].astype(F32)
    angle = spread(jnp.where(row8, my_rows + start, 0.0), HD) * freq[...]
    lane_sign = jnp.where(lax.broadcasted_iota(jnp.int32, (1, HD), 1) < 64, -1.0, 1.0)
    trig[0, :SEL] = jnp.cos(angle)
    trig[1, :SEL] = jnp.sin(angle) * lane_sign
    shift = jnp.broadcast_to(freq[...] * start, (8, HD))
    trig[0, SEL:] = jnp.where(values, 1.0, jnp.cos(shift))
    trig[1, SEL:] = jnp.where(values, 0.0, jnp.sin(shift) * lane_sign)
    kz_a, kx_a = settle(0, ra)
    multiply(0, acc, 0)
    send_far(2)
    send_far(3)
    send_near(0)
    send_near(1)
    waits(sq_y)
    sqz[...] = sqs[0] + sqr[1] + sqr[2] + sqr[3]
    sq_z = [push(sqz, sqzr.at[4 - d], zpeer(d)) for d in (1, 3, 2)]
    rb = route_store(1, fb)
    pass_on(0, kz_a, kx_a)
    fc = forward_store(2, sc)
    kz_b, kx_b = settle(1, rb)
    send_near(2)
    pass_far(0, kz_a, kx_a)
    pz = [send_z(0)]
    rc = route_store(2, fc)
    send_near(3)
    pass_on(1, kz_b, kx_b)
    pz.append(send_z(1))
    kz_c, kx_c = settle(2, rc)
    pass_far(1, kz_b, kx_b)

    waits(sq_z)
    squares = sqz[...] + sqzr[1] + sqzr[2] + sqzr[3]
    own = lax.broadcasted_iota(jnp.int32, (8, 128), 0) == z
    inv = lax.rsqrt(spread(jnp.where(own, squares, 0.0), HD)[:SEL] / D + EPS)

    def summed(lo):
        cols = pl.ds(lo, HD)
        v = (total[z, :, cols] + precv[0, z, :, cols].astype(F32)
             + precv[1, z, :, cols].astype(F32))
        for d in (1, 2, 3):
            v = v + zrecv[d, :, cols].astype(F32)
        return v * inv

    waits(pz[0])
    fr[kind, 0] = turned(
        summed(0), jnp.where(values, 1.0, trig[0, :SEL]),
        jnp.where(values, 0.0, trig[1, :SEL])).astype(BF16)
    fz = {4 - d: push(fr.at[kind, 0], fr.at[kind, 4 - d], zpeer(d)) for d in (1, 3, 2)}
    fx = [push(fr.at[kind, 0], fr.at[kind, 0], partner)]
    pass_on(2, kz_c, kx_c)
    pz.append(send_z(2))
    qy = []

    def send_queries(k):
        waits(pz[k + 1])
        for j in (0, 1):
            q[k, j * SEL:(j + 1) * SEL] = turned(
                summed(HD + (2 * k + j) * HD), trig[0, :SEL], trig[1, :SEL]).astype(BF16)
        mine = q.at[k, pl.ds(0, QC)]
        qy.append([push(mine, q.at[k, pl.ds((4 - d) * QC, QC)], ypeer(d)) for d in (1, 3, 2)])

    send_queries(0)
    pass_far(2, kz_c, kx_c)
    for r in (3, 1, 2):
        fz[r].wait_recv()
        fx.append(push(fr.at[kind, r], fr.at[kind, r], partner))
    pz.append(send_z(3))
    send_queries(1)

    waits(kx_a)
    waits(kx_b)
    waits(kx_c)
    waits(fx)
    for r in range(4):
        group = rows[pl.ds(y * 4 + (z + r) % 4, 1), :]
        hit = lax.broadcasted_iota(jnp.int32, (L, SEL), 0) == group
        hot = jnp.where(hit, 1.0, 0.0)
        taken = jnp.max(hot, axis=1, keepdims=True) > 0.0
        hot = hot.astype(BF16)
        for k in (0, 1):
            placed = jnp.dot(hot, fr[k, r], preferred_element_type=F32)
            patched = jnp.where(taken, placed, kvc[k, r].astype(F32))
            if r == 0:
                first_kv[k] = patched.astype(BF16)
            if k == 0:
                keys[r] = patched.astype(BF16)
            else:
                vt[:, r * L:(r + 1) * L] = patched.T.astype(BF16)
    blended[...] = first_kv[kind]

    lane = lax.broadcasted_iota(jnp.int32, (1, TQ), 1)
    first = jnp.full((1, TQ), positions[y * 4 + z], jnp.int32)
    for d in (1, 2, 3):
        first = jnp.where(lane >= d * QC, positions[((y + d) % 4) * 4 + z], first)
    tiled = (lax.broadcasted_iota(jnp.int32, (SEL, TQ), 1) % SEL
             == lax.broadcasted_iota(jnp.int32, (SEL, TQ), 0))
    limit = lax.dot_general(
        jnp.where(row8, my_rows, 0.0), jnp.where(tiled, 1.0, 0.0), (((1,), (0,)), ((), ())),
        precision=lax.Precision.HIGHEST, preferred_element_type=F32)[:1]
    limit = jnp.where(lane < QC, limit, float(L))
    hidden = [positions[y * 4 + (z + e) % 4] > first for e in range(4)]

    def attend(k):
        waits(qy[k])
        block = q[k]
        top = jnp.full((1, TQ), MASKED, F32)
        for e in range(4):
            sc = lax.dot_general(
                keys[e], block, (((1,), (1,)), ((), ())), preferred_element_type=F32)
            if e == 0:
                line = lax.broadcasted_iota(jnp.int32, (L, TQ), 0).astype(F32)
                sc = jnp.where(line <= limit, sc, MASKED)
            sbuf[e] = sc
            top = jnp.maximum(
                top, jnp.where(hidden[e], MASKED, jnp.max(sc, axis=0, keepdims=True)))
        top = top * SCALE2
        weight = jnp.zeros((1, TQ), F32)
        for e in range(4):
            base = top + jnp.where(hidden[e], 1e30, 0.0)
            p = jnp.exp2(sbuf[e] * SCALE2 - base)
            weight = weight + jnp.sum(p, axis=0, keepdims=True)
            pbuf[e] = p.astype(BF16)
        num = jnp.dot(vt[...], pbuf[...].reshape(4 * L, TQ), preferred_element_type=F32)
        some = weight > 0.0
        safe = jnp.where(some, weight, 1.0)
        o[k] = (num * (1.0 / safe)).T.astype(BF16)
        logs = jnp.broadcast_to(jnp.where(some, top + jnp.log2(safe), MASKED), (8, TQ))
        for d in range(4):
            moved = pltpu.roll(logs, TQ - d * QC, 1) if d else logs
            lse[k, d] = moved[:, :256]
        got = {}
        for d in (2, 1, 3):
            got[4 - d] = [push(o.at[k, pl.ds(d * QC, QC)], orecv.at[k, 4 - d], ypeer(d)),
                          push(lse.at[k, d], lrecv.at[k, 4 - d], ypeer(d))]
        return got

    def merge(k, got):
        for r in (1, 3, 2):
            waits(got[r])
        logs = [lse[k, 0, :1]] + [lrecv[k, r, :1] for r in (1, 2, 3)]
        top = jnp.maximum(jnp.maximum(logs[0], logs[1]), jnp.maximum(logs[2], logs[3]))
        share = [jnp.exp2(v - top) for v in logs]
        whole = share[0] + share[1] + share[2] + share[3]
        line = lax.broadcasted_iota(jnp.int32, (8, 256), 0) == 0
        merged = jnp.zeros((QC, HD), F32)
        for r in range(4):
            part = o[k, :QC] if r == 0 else orecv[k, r]
            col = spread(jnp.where(line, share[r] / whole, 0.0), HD)[:QC]
            merged = merged + part.astype(F32) * col
        for j in (0, 1):
            lo = (2 * k + j) * HD
            ag[0, z, :, lo:lo + HD] = merged[j * SEL:(j + 1) * SEL].astype(BF16)

    zs, ups, dns, fw = {}, {}, {}, {}

    def block_of(r, k, d):
        return ag.at[r, (z + d) % 4, :, pl.ds(k * 256, 256)]

    def send_y(k, d):
        ups[k, d] = push(block_of(0, k, d), block_of(3, k, d), ypeer(1))
        dns[k, d] = push(block_of(0, k, d), block_of(1, k, d), ypeer(3))

    def gather_start(k, got):
        merge(k, got)
        mine = block_of(0, k, 0)
        zs[k, 1] = push(mine, mine, zpeer(1))
        zs[k, 3] = push(mine, mine, zpeer(3))
        send_y(k, 0)
        zs[k, 2] = push(mine, mine, zpeer(2))

    def gather_z(k):
        for d in (3, 1, 2):
            zs[k, 4 - d].wait_recv()
            send_y(k, d)

    def gather_far(k):
        for d in (0, 3, 1, 2):
            ups[k, d].wait_recv()
            dns[k, d].wait_recv()
            if d in (0, 3):
                fw[k, d] = push(block_of(3, k, d), block_of(2, k, d), ypeer(1))
            else:
                fw[k, d] = push(block_of(1, k, d), block_of(2, k, d), ypeer(3))

    def multiply_out(r, c):
        cols = pl.ds(c * OC, OC)
        a = jnp.dot(ag[r].reshape(4 * SEL, 768), wo[:, cols], preferred_element_type=F32)
        a = a.reshape(4, SEL, OC).astype(BF16)
        for g in range(4):
            prod[r, c, g % 2, g // 2] = a[g]
        return push(prod.at[r, c, 1 - core], crecv.at[r, c], twin)

    def send_zl(r, c, copy):
        copy.wait_recv()
        csum[r, c] = (prod[r, c, core].astype(F32) + crecv[r, c].astype(F32)).astype(BF16)
        return push(csum.at[r, c, 1 - zl], zlrecv.at[r, c], pair)

    def x_copy(r, c, slot):
        return pltpu.make_async_remote_copy(
            src_ref=xsum.at[r, c], dst_ref=xrecv.at[slot, c], send_sem=ssem.at[XBASE + 2 * r + c],
            recv_sem=rsem.at[XBASE + 2 * slot + c], device_id=xpeer(4 - slot),
            device_id_type=MESH)

    def away(r):
        return (y + r + 4 - x) % 4

    def send_x(r, c, copy):
        copy.wait_recv()
        xsum[r, c] = (csum[r, c, zl].astype(F32) + zlrecv[r, c].astype(F32)).astype(BF16)

        @pl.when(away(r) != 0)
        def _():
            x_copy(r, c, (4 - away(r)) % 4).start()

    g0 = attend(0)
    send_queries(2)
    g1 = attend(1)
    gather_start(0, g0)
    g2 = attend(2)
    gather_z(0)
    gather_start(1, g1)
    gather_z(1)
    gather_start(2, g2)
    gather_far(0)
    gather_z(2)
    gather_far(1)
    local[3 + NP].wait()
    tw = {(0, c): multiply_out(0, c) for c in (0, 1)}
    gather_far(2)
    zz = {}
    for r in (1, 3):
        for c in (0, 1):
            tw[r, c] = multiply_out(r, c)
    for r in (0, 1, 3):
        for c in (0, 1):
            zz[r, c] = send_zl(r, c, tw[r, c])
    for c in (0, 1):
        send_x(0, c, zz[0, c])
    for k in range(3):
        for d in (0, 3, 1, 2):
            fw[k, d].wait_recv()
    for c in (0, 1):
        tw[2, c] = multiply_out(2, c)
    for r in (1, 3):
        for c in (0, 1):
            send_x(r, c, zz[r, c])
    for c in (0, 1):
        zz[2, c] = send_zl(2, c, tw[2, c])
    for c in (0, 1):
        send_x(2, c, zz[2, c])
    home = (x + 4 - y) % 4
    for c in (0, 1):
        v = xsum[home, c].astype(F32)
        for slot in (1, 2, 3):
            x_copy(0, c, slot).wait_recv()
            v = v + xrecv[slot, c].astype(F32)
        mixed[:, c * OC:(c + 1) * OC] = v.astype(BF16)
    for r in range(4):
        @pl.when(away(r) != 0)
        def _():
            for c in (0, 1):
                x_copy(r, c, 1).wait_send()
    for c in sent:
        c.wait_send()
    assert ids[0] <= XBASE


VM = pl.BlockSpec(memory_space=pltpu.VMEM)
SM = pl.BlockSpec(memory_space=pltpu.SMEM)
ANY = pl.BlockSpec(memory_space=pl.ANY)
FREQ = (THETA ** (-2.0 * (np.arange(HD) % (HD // 2)) / HD)).astype(np.float32)[None]


def shards(store, owners, positions, sel_rows, sel_hidden, norm_gain, w_query, w_keyval, w_out):
    blended, mixed = pl.pallas_call(
        sublayer,
        name="sublayer",
        out_shape=(
            jax.ShapeDtypeStruct((L, HD), BF16),
            jax.ShapeDtypeStruct((SEL, 768), BF16),
        ),
        in_specs=[SM, SM, VM, VM, VM, ANY, ANY, ANY, ANY, ANY],
        out_specs=(VM, VM),
        scratch_shapes=[
            pltpu.VMEM((16, SEL, 768), BF16),
            pltpu.VMEM((768, 768), BF16),
            pltpu.VMEM((768, HD), BF16),
            pltpu.VMEM((768, 768), BF16),
            *[pltpu.VMEM((4, 4, n, HD), BF16) for _, n in PARTS],
            pltpu.VMEM((4, L, HD), BF16),
            pltpu.VMEM((4, L, HD), BF16),
            pltpu.VMEM((1, 4, SEL, PW), BF16),
            pltpu.VMEM((2, 2, SEL, PW), BF16),
            pltpu.VMEM((3, 4, SEL, PW), F32),
            pltpu.VMEM((2, 4, SEL, PW), BF16),
            pltpu.VMEM((2, 4, SEL, PW), BF16),
            pltpu.VMEM((4, SEL, PW), BF16),
            pltpu.VMEM((4, SEL, PW), BF16),
            pltpu.VMEM((4, 8, 128), F32),
            pltpu.VMEM((4, 8, 128), F32),
            pltpu.VMEM((8, 128), F32),
            pltpu.VMEM((4, 8, 128), F32),
            pltpu.VMEM((2, SEL + 8, HD), F32),
            pltpu.VMEM((2, 4, L, HD), BF16),
            pltpu.VMEM((2, 4, SEL, HD), BF16),
            pltpu.VMEM((4, L, HD), BF16),
            pltpu.VMEM((HD, 4 * L), BF16),
            pltpu.VMEM((2, L, HD), BF16),
            pltpu.VMEM((3, TQ, HD), BF16),
            pltpu.VMEM((4, L, TQ), F32),
            pltpu.VMEM((4, L, TQ), BF16),
            pltpu.VMEM((3, TQ, HD), BF16),
            pltpu.VMEM((3, 4, 8, 256), F32),
            pltpu.VMEM((3, 4, QC, HD), BF16),
            pltpu.VMEM((3, 4, 8, 256), F32),
            pltpu.VMEM((4, 4, SEL, 768), BF16),
            pltpu.VMEM((4, 2, 2, 2, SEL, OC), BF16),
            pltpu.VMEM((4, 2, 2, SEL, OC), BF16),
            pltpu.VMEM((4, 2, 2, SEL, OC), BF16),
            pltpu.VMEM((4, 2, SEL, OC), BF16),
            pltpu.VMEM((4, 2, SEL, OC), BF16),
            pltpu.VMEM((4, 2, SEL, OC), BF16),
            pltpu.SemaphoreType.DMA((SEMS,)),
            pltpu.SemaphoreType.DMA((SEMS,)),
            pltpu.SemaphoreType.DMA((4 + NP,)),
        ],
        compiler_params=pltpu.CompilerParams(
            collective_id=0, has_side_effects=True, vmem_limit_bytes=52 * 2**20),
    )(owners, positions, sel_rows, norm_gain, jnp.asarray(FREQ),
      sel_hidden, w_query, w_keyval, store, w_out)
    return blended[None], mixed[None]


def solution(mesh):
    return jax.shard_map(
        shards,
        mesh=mesh,
        in_specs=(
            P("section", None, "tensor"),
            P(),
            P(),
            P(),
            P(None, None, "section"),
            P("section"),
            P("section", "tensor"),
            P("section", "tensor"),
            P("tensor", "section"),
        ),
        out_specs=(P("section", None, "tensor"), P("tensor", None, "section")),
        check_vma=False,
    )
```

```python
import math

import jax
import jax.numpy as jnp
import numpy as np
from jax import lax
from jax.experimental import pallas as pl
from jax.experimental.pallas import tpu as pltpu
from jax.sharding import PartitionSpec as P

D = 12288
HD = 128
HALF = 6
L = 640
SEL = 96
THETA = 1000000.0
EPS = 1e-05
MASKED = -1e30
MESH = pl.DeviceIdType.MESH
F32 = jnp.float32
BF16 = jnp.bfloat16
PW = 896
QN = HALF * SEL
QC = 2 * SEL
TQ = 4 * QC
PARTS = [(0, 192), (192, 256), (448, 192)]
NP = len(PARTS)
OC = 384
SCALE2 = math.log2(math.e) / math.sqrt(HD)
CHUNKS = [(0, 128), (128, 256), (384, 256), (640, 256)]
XBASE = 190
ORDER = (
    "s0", "a0", "s1", "m2", "f0", "f1", "s2", "r0", "m3", "m0", "F0", "r1", "F1", "m1",
    "f2", "t0", "r2", "N1", "t1", "N0", "o0", "t2", "F2", "Z0", "o1", "F3", "N2", "q0",
    "Z1", "o2", "E0", "p2", "p0", "N3", "Z2", "p1", "G0", "Q0", "Z3", "P0", "Q1", "A0",
    "Q2", "A1", "M0", "A2", "M1", "H0", "M2", "H1", "I1", "I0", "I2", "H2", "K1", "K0",
    "R0", "K2",
)
SEMS = 210


def spread(vec, lanes):
    return lax.dot_general(
        vec, jnp.ones((8, lanes), F32), (((0,), (0,)), ((), ())),
        precision=lax.Precision.HIGHEST, preferred_element_type=F32,
    )


def turned(v, c, sn):
    return v * c + pltpu.roll(v, 64, 1) * sn


def sublayer(owners, positions, rows, gain, freq, h_any, wq_any, wkv_any, store, wo_any,
             blended, mixed,
             h, wq, wkv, wo, st0, st1, st2, stsend, strecv, p2, p2r, acc, psend, precv, zsend,
             zrecv, sqs, sqr, sqz, sqzr, scale, trig, kvc, fr, keys, vt, first_kv, q, sbuf, pbuf, o, lse,
             orecv, lrecv, ag, prod, crecv, csum, zlrecv, xsum, xrecv, xwide, fin, ssem, rsem, lsem):
    s = lax.axis_index("section")
    t = lax.axis_index("tensor")
    y, z = s // 4, s % 4
    x, zl, core = t // 4, (t // 2) % 2, t % 2
    kind = t // 8
    values = kind == 1

    def ypeer(d):
        return {"section": ((y + d) % 4) * 4 + z}

    def zpeer(d):
        return {"section": y * 4 + (z + d) % 4}

    def xpeer(d):
        return {"tensor": ((x + d) % 4) * 4 + t % 4}

    twin = {"tensor": x * 4 + zl * 2 + 1 - core}
    pair = {"tensor": x * 4 + (1 - zl) * 2 + core}
    partner = xpeer(2)
    sent = []
    ids = [0]

    def push(src, dst, dev):
        i = ids[0]
        ids[0] += 1
        c = pltpu.make_async_remote_copy(
            src_ref=src, dst_ref=dst, send_sem=ssem.at[i], recv_sem=rsem.at[i],
            device_id=dev, device_id_type=MESH)
        c.start()
        sent.append(c)
        return c

    def waits(copies):
        for c in copies:
            c.wait_recv()

    st = [st0, st1, st2]
    local = []

    def fetch(src, dst):
        c = pltpu.make_async_copy(src, dst, lsem.at[len(local)])
        c.start()
        local.append(c)

    fetch(h_any, h)
    fetch(wq_any, wq)
    fetch(wkv_any, wkv)
    for k, (lo, n) in enumerate(PARTS):
        fetch(store.at[:, pl.ds(lo, n)], st[k].at[y])
    fetch(wo_any, wo)

    peers = [f(d) for f in (ypeer, zpeer, xpeer) for d in (1, 2, 3)] + [twin, pair]
    barrier = pltpu.get_barrier_semaphore()
    for peer in peers:
        pl.semaphore_signal(barrier, inc=1, device_id=peer, device_id_type=MESH)
    pl.semaphore_wait(barrier, len(peers))

    def send_store(k):
        src = store.at[:, pl.ds(*PARTS[k])]
        return [push(src, st[k].at[y], ypeer(1)), push(src, st[k].at[y], ypeer(3))]

    def forward_store(k, copies):
        waits(copies)
        below, above = (y + 3) % 4, (y + 1) % 4
        a, b = st[k].at[below, pl.ds(0, 2)], st[k].at[above, pl.ds(2, 2)]
        return [push(a, a, ypeer(1)), push(b, b, ypeer(3))]

    def picked(k, d):
        slot = owners[y * 4 + (z + d) % 4]
        here = ((slot >> 2) & 3) == z
        block = st[k][slot >> 4, slot & 3]
        return jnp.where(here, block, jnp.zeros_like(block))

    def route_store(k, copies):
        local[3 + k].wait()
        waits(copies)
        part = pl.ds(*PARTS[k])
        out = []
        for d in (1, 3, 2):
            stsend[d, part] = picked(k, d)
            out.append(push(stsend.at[d, part], strecv.at[4 - d, part], zpeer(d)))
        return out

    ones8 = jnp.ones((8, 128), F32)
    gains = gain[...].astype(F32).reshape(1, 768)

    def multiply(d, out, i):
        hf = h[pl.ds(((y + d) % 4) * 4, 4)].astype(F32).reshape(4 * SEL, 768)
        hg = (hf * gains).astype(BF16)
        a = jnp.dot(hg, wkv[...], preferred_element_type=F32)
        b = jnp.dot(hg, wq[...], preferred_element_type=F32)
        out[i, :, :, :HD] = a.reshape(4, SEL, HD).astype(out.dtype)
        out[i, :, :, HD:] = b.reshape(4, SEL, 768).astype(out.dtype)
        sq = hf * hf
        part = sq[:, :128]
        for k in range(1, 6):
            part = part + sq[:, k * 128:(k + 1) * 128]
        sqs[d] = jnp.zeros((8, 128), F32)
        for g in range(4):
            row = lax.dot_general(
                ones8, part[g * SEL:(g + 1) * SEL], (((1,), (1,)), ((), ())),
                precision=lax.Precision.HIGHEST, preferred_element_type=F32)
            sqs[d, g:g + 1, :SEL] = row[:1]

    up2, dn2, up1, dn1 = {}, {}, {}, {}

    def send_far(k):
        cols = pl.ds(*CHUNKS[k])
        up2[k] = push(p2.at[0, pl.ds(0, 2), :, cols], p2r.at[0, :, :, cols], ypeer(1))
        dn2[k] = push(p2.at[0, pl.ds(2, 2), :, cols], p2r.at[1, :, :, cols], ypeer(3))

    def send_near(k):
        cols = pl.ds(*CHUNKS[k])
        up2[k].wait_recv()
        psend[0, :2, :, cols] = (acc[1, :2, :, cols] + p2r[0, :, :, cols].astype(F32)).astype(BF16)
        psend[0, 2:, :, cols] = acc[1, 2:, :, cols].astype(BF16)
        up1[k] = push(psend.at[0, :, :, cols], precv.at[0, :, :, cols], ypeer(1))
        dn2[k].wait_recv()
        psend[1, 2:, :, cols] = (acc[2, 2:, :, cols] + p2r[1, :, :, cols].astype(F32)).astype(BF16)
        psend[1, :2, :, cols] = acc[2, :2, :, cols].astype(BF16)
        dn1[k] = push(psend.at[1, :, :, cols], precv.at[1, :, :, cols], ypeer(3))

    total = acc.at[0]

    def send_z(k):
        cols = pl.ds(*CHUNKS[k])
        up1[k].wait_recv()
        dn1[k].wait_recv()
        out = []
        for d in (1, 3, 2):
            g = (z + d) % 4
            zsend[d, :, cols] = (total[g, :, cols] + precv[0, g, :, cols].astype(F32)
                                 + precv[1, g, :, cols].astype(F32)).astype(BF16)
            out.append(push(zsend.at[d, :, cols], zrecv.at[4 - d, :, cols], zpeer(d)))
        return out

    def settle(k, copies):
        cached = picked(k, 0)
        waits(copies)
        part = pl.ds(*PARTS[k])
        for d in (1, 2, 3):
            cached = cached + strecv[d, part]
        kvc[kind, 0, part] = turned(
            cached.astype(F32), trig[0, SEL:SEL + 1], trig[1, SEL:SEL + 1]).astype(BF16)
        mine = kvc.at[kind, 0, part]
        out = {4 - d: push(mine, kvc.at[kind, 4 - d, part], zpeer(d)) for d in (1, 3)}
        return out, [push(mine, mine, partner)]

    def pass_on(k, kz, kx):
        lo, n = PARTS[k]
        part = pl.ds(lo, n)
        for r, half, to in ((1, lo, 3), (3, lo + n // 2, 1)):
            kz[r].wait_recv()
            half = pl.ds(half, n // 2)
            kz[r + 4] = push(kvc.at[kind, r, half], kvc.at[kind, 2, half], zpeer(to))
            kx.append(push(kvc.at[kind, r, part], kvc.at[kind, r, part], partner))

    def pass_far(k, kz, kx):
        part = pl.ds(*PARTS[k])
        kz[5].wait_recv()
        kz[7].wait_recv()
        kx.append(push(kvc.at[kind, 2, part], kvc.at[kind, 2, part], partner))

    row8 = lax.broadcasted_iota(jnp.int32, (8, SEL), 0) == 0
    start = positions[s].astype(F32)
    my_rows = rows[pl.ds(s, 1), :].astype(F32)

    def angles():
        angle = spread(jnp.where(row8, my_rows + start, 0.0), HD) * freq[...]
        lane_sign = jnp.where(lax.broadcasted_iota(jnp.int32, (1, HD), 1) < 64, -1.0, 1.0)
        trig[0, :SEL] = jnp.cos(angle)
        trig[1, :SEL] = jnp.sin(angle) * lane_sign
        shift = jnp.broadcast_to(freq[...] * start, (8, HD))
        trig[0, SEL:] = jnp.where(values, 1.0, jnp.cos(shift))
        trig[1, SEL:] = jnp.where(values, 0.0, jnp.sin(shift) * lane_sign)

    sends, fars, routes, kz, kx, pz, qy = {}, {}, {}, {}, {}, {}, {}
    sq_y, sq_z, fz, fx = [], [], {}, []

    def do_send(k):
        sends[k] = send_store(k)

    def do_forward(k):
        fars[k] = forward_store(k, sends[k])

    def do_route(k):
        routes[k] = route_store(k, fars[k])

    def do_settle(k):
        kz[k], kx[k] = settle(k, routes[k])

    def do_multiply(d):
        if d == 2:
            for c in local[:3]:
                c.wait()
            multiply(2, p2, 0)
        else:
            multiply(d, acc, {1: 1, 3: 2, 0: 0}[d])
        if d:
            sq_y.append(push(sqs.at[d], sqr.at[4 - d], ypeer(d)))

    def do_z(k):
        pz[k] = send_z(k)

    def do_squares(_):
        waits(sq_y)
        sqz[...] = sqs[0] + sqr[1] + sqr[2] + sqr[3]
        sq_z.extend(push(sqz, sqzr.at[4 - d], zpeer(d)) for d in (1, 3, 2))

    def factor():
        waits(sq_z)
        squares = sqz[...] + sqzr[1] + sqzr[2] + sqzr[3]
        own = lax.broadcasted_iota(jnp.int32, (8, 128), 0) == z
        return lax.rsqrt(spread(jnp.where(own, squares, 0.0), HD)[:SEL] / D + EPS)

    def summed(lo):
        cols = pl.ds(lo, HD)
        v = (total[z, :, cols] + precv[0, z, :, cols].astype(F32)
             + precv[1, z, :, cols].astype(F32))
        for d in (1, 2, 3):
            v = v + zrecv[d, :, cols].astype(F32)
        return v * scale[...]

    def do_fresh(_):
        scale[...] = factor()
        waits(pz[0])
        fr[kind, 0] = turned(
            summed(0), jnp.where(values, 1.0, trig[0, :SEL]),
            jnp.where(values, 0.0, trig[1, :SEL])).astype(BF16)
        for d in (1, 3, 2):
            fz[4 - d] = push(fr.at[kind, 0], fr.at[kind, 4 - d], zpeer(d))
        fx.append(push(fr.at[kind, 0], fr.at[kind, 0], partner))

    def do_fresh_over(_):
        for r in (3, 1, 2):
            fz[r].wait_recv()
            fx.append(push(fr.at[kind, r], fr.at[kind, r], partner))

    def send_queries(k):
        waits(pz[k + 1])
        for j in (0, 1):
            q[k, j * SEL:(j + 1) * SEL] = turned(
                summed(HD + (2 * k + j) * HD), trig[0, :SEL], trig[1, :SEL]).astype(BF16)
        mine = q.at[k, pl.ds(0, QC)]
        qy[k] = [push(mine, q.at[k, pl.ds((4 - d) * QC, QC)], ypeer(d)) for d in (1, 3, 2)]

    def do_patch(_):
        for copies in kx.values():
            waits(copies)
        waits(fx)
        for r in range(4):
            group = rows[pl.ds(y * 4 + (z + r) % 4, 1), :]
            hit = lax.broadcasted_iota(jnp.int32, (L, SEL), 0) == group
            hot = jnp.where(hit, 1.0, 0.0)
            taken = jnp.max(hot, axis=1, keepdims=True) > 0.0
            hot = hot.astype(BF16)
            for k in (0, 1):
                placed = jnp.dot(hot, fr[k, r], preferred_element_type=F32)
                patched = jnp.where(taken, placed, kvc[k, r].astype(F32))
                if r == 0:
                    first_kv[k] = patched.astype(BF16)
                if k == 0:
                    keys[r] = patched.astype(BF16)
                else:
                    vt[:, r * L:(r + 1) * L] = patched.T.astype(BF16)
        blended[...] = first_kv[kind]

    lane = lax.broadcasted_iota(jnp.int32, (1, TQ), 1)
    first = jnp.full((1, TQ), positions[y * 4 + z], jnp.int32)
    for d in (1, 2, 3):
        first = jnp.where(lane >= d * QC, positions[((y + d) % 4) * 4 + z], first)
    tiled = (lax.broadcasted_iota(jnp.int32, (SEL, TQ), 1) % SEL
             == lax.broadcasted_iota(jnp.int32, (SEL, TQ), 0))
    limit = lax.dot_general(
        jnp.where(row8, my_rows, 0.0), jnp.where(tiled, 1.0, 0.0), (((1,), (0,)), ((), ())),
        precision=lax.Precision.HIGHEST, preferred_element_type=F32)[:1]
    limit = jnp.where(lane < QC, limit, float(L))
    hidden = [positions[y * 4 + (z + e) % 4] > first for e in range(4)]

    def attend(k):
        waits(qy[k])
        block = q[k]
        top = jnp.full((1, TQ), MASKED, F32)
        for e in range(4):
            sc = lax.dot_general(
                keys[e], block, (((1,), (1,)), ((), ())), preferred_element_type=F32)
            if e == 0:
                line = lax.broadcasted_iota(jnp.int32, (L, TQ), 0).astype(F32)
                sc = jnp.where(line <= limit, sc, MASKED)
            sbuf[e] = sc
            top = jnp.maximum(
                top, jnp.where(hidden[e], MASKED, jnp.max(sc, axis=0, keepdims=True)))
        top = top * SCALE2
        weight = jnp.zeros((1, TQ), F32)
        for e in range(4):
            base = top + jnp.where(hidden[e], 1e30, 0.0)
            p = jnp.exp2(sbuf[e] * SCALE2 - base)
            weight = weight + jnp.sum(p, axis=0, keepdims=True)
            pbuf[e] = p.astype(BF16)
        num = jnp.dot(vt[...], pbuf[...].reshape(4 * L, TQ), preferred_element_type=F32)
        some = weight > 0.0
        safe = jnp.where(some, weight, 1.0)
        o[k] = (num * (1.0 / safe)).T.astype(BF16)
        logs = jnp.broadcast_to(jnp.where(some, top + jnp.log2(safe), MASKED), (8, TQ))
        for d in range(4):
            moved = pltpu.roll(logs, TQ - d * QC, 1) if d else logs
            lse[k, d] = moved[:, :256]
        got = {}
        for d in (2, 1, 3):
            got[4 - d] = [push(o.at[k, pl.ds(d * QC, QC)], orecv.at[k, 4 - d], ypeer(d)),
                          push(lse.at[k, d], lrecv.at[k, 4 - d], ypeer(d))]
        return got

    def merge(k, got):
        for r in (1, 3, 2):
            waits(got[r])
        logs = [lse[k, 0, :1]] + [lrecv[k, r, :1] for r in (1, 2, 3)]
        top = jnp.maximum(jnp.maximum(logs[0], logs[1]), jnp.maximum(logs[2], logs[3]))
        share = [jnp.exp2(v - top) for v in logs]
        whole = share[0] + share[1] + share[2] + share[3]
        line = lax.broadcasted_iota(jnp.int32, (8, 256), 0) == 0
        merged = jnp.zeros((QC, HD), F32)
        for r in range(4):
            part = o[k, :QC] if r == 0 else orecv[k, r]
            col = spread(jnp.where(line, share[r] / whole, 0.0), HD)[:QC]
            merged = merged + part.astype(F32) * col
        for j in (0, 1):
            lo = (2 * k + j) * HD
            ag[0, z, :, lo:lo + HD] = merged[j * SEL:(j + 1) * SEL].astype(BF16)

    zs, ups, dns, fw = {}, {}, {}, {}

    def block_of(r, k, d):
        return ag.at[r, (z + d) % 4, :, pl.ds(k * 256, 256)]

    def send_y(k, d):
        ups[k, d] = push(block_of(0, k, d), block_of(3, k, d), ypeer(1))
        dns[k, d] = push(block_of(0, k, d), block_of(1, k, d), ypeer(3))

    def gather_start(k, got):
        merge(k, got)
        mine = block_of(0, k, 0)
        zs[k, 1] = push(mine, mine, zpeer(1))
        zs[k, 3] = push(mine, mine, zpeer(3))
        send_y(k, 0)
        zs[k, 2] = push(mine, mine, zpeer(2))

    def gather_z(k, blocks):
        for d in blocks:
            zs[k, 4 - d].wait_recv()
            send_y(k, d)

    def gather_far(k):
        for d in (0, 3, 1, 2):
            ups[k, d].wait_recv()
            dns[k, d].wait_recv()
            if d in (0, 3):
                fw[k, d] = push(block_of(3, k, d), block_of(2, k, d), ypeer(1))
            else:
                fw[k, d] = push(block_of(1, k, d), block_of(2, k, d), ypeer(3))

    def multiply_out(r, c):
        cols = pl.ds(c * OC, OC)
        a = jnp.dot(ag[r].reshape(4 * SEL, 768), wo[:, cols], preferred_element_type=F32)
        a = a.reshape(4, SEL, OC).astype(BF16)
        for g in range(4):
            prod[r, c, g % 2, g // 2] = a[g]
        return push(prod.at[r, c, 1 - core], crecv.at[r, c], twin)

    def send_zl(r, c, copy):
        copy.wait_recv()
        csum[r, c] = (prod[r, c, core].astype(F32) + crecv[r, c].astype(F32)).astype(BF16)
        return push(csum.at[r, c, 1 - zl], zlrecv.at[r, c], pair)

    wide = (1, 3)

    def x_copy(r, c, slot):
        src, dst = (csum, xwide) if r in wide else (xsum, xrecv)
        return pltpu.make_async_remote_copy(
            src_ref=src.at[r, c], dst_ref=dst.at[slot, c], send_sem=ssem.at[XBASE + 2 * r + c],
            recv_sem=rsem.at[XBASE + 2 * slot + c], device_id=xpeer(4 - slot),
            device_id_type=MESH)

    def away(r):
        return (y + r + 4 - x) % 4

    def send_x(r, c, copy):
        copy.wait_recv()
        if r in wide:
            csum[r, c] = (prod[r, c, core].astype(F32) + crecv[r, c].astype(F32)).astype(BF16)
        else:
            xsum[r, c] = (csum[r, c, zl].astype(F32) + zlrecv[r, c].astype(F32)).astype(BF16)

        @pl.when(away(r) != 0)
        def _():
            x_copy(r, c, (4 - away(r)) % 4).start()

    parts, tw = {}, {}

    def do_product(r):
        if not tw:
            local[3 + NP].wait()
        for c in (0, 1):
            tw[r, c] = multiply_out(r, c)

    def do_attend(k):
        parts[k] = attend(k)

    steps = {
        "s": do_send, "f": do_forward, "r": do_route, "t": do_settle,
        "o": lambda k: pass_on(k, kz[k], kx[k]), "p": lambda k: pass_far(k, kz[k], kx[k]),
        "m": do_multiply, "F": send_far, "N": send_near, "Z": do_z, "a": lambda _: angles(),
        "q": do_squares, "E": do_fresh, "G": do_fresh_over, "Q": send_queries, "P": do_patch,
        "A": do_attend, "M": lambda k: gather_start(k, parts[k]),
        "H": lambda k: gather_z(k, (3, 1)), "I": lambda k: gather_z(k, (2,)), "K": gather_far,
        "R": do_product,
    }
    for step in ORDER:
        steps[step[0]](int(step[1]))
    zz = {}
    for c in (0, 1):
        zz[0, c] = send_zl(0, c, tw[0, c])
    do_product(1)
    do_product(3)
    for r in wide:
        for c in (0, 1):
            send_x(r, c, tw[r, c])
    for c in (0, 1):
        send_x(0, c, zz[0, c])
    for k in range(3):
        for d in (0, 3, 1, 2):
            fw[k, d].wait_recv()
    do_product(2)
    for c in (0, 1):
        zz[2, c] = send_zl(2, c, tw[2, c])
    for c in (0, 1):
        send_x(2, c, zz[2, c])
    home = (x + 4 - y) % 4

    @pl.when(home % 2 == 0)
    def _():
        for c in (0, 1):
            v = xsum[home, c].astype(F32)
            for slot in (1, 2, 3):
                x_copy(0, c, slot).wait_recv()
                v = v + xrecv[slot, c].astype(F32)
            mixed[:, c * OC:(c + 1) * OC] = v.astype(BF16)

    @pl.when(home % 2 == 1)
    def _():
        last = []
        for c in (0, 1):
            for slot in (1, 2, 3):
                x_copy(1, c, slot).wait_recv()
            both = []
            for k in (1 - zl, zl):
                v = csum[home, c, k].astype(F32)
                for slot in (1, 2, 3):
                    v = v + xwide[slot, c, k].astype(F32)
                both.append(v)
            xsum[1, c] = both[0].astype(BF16)
            copy = pltpu.make_async_remote_copy(
                src_ref=xsum.at[1, c], dst_ref=zlrecv.at[1, c], send_sem=ssem.at[XBASE + 8 + c],
                recv_sem=rsem.at[XBASE + 8 + c], device_id=pair, device_id_type=MESH)
            copy.start()
            last.append(copy)
            fin[c] = both[1]
        for c in (0, 1):
            last[c].wait_recv()
            mixed[:, c * OC:(c + 1) * OC] = (fin[c] + zlrecv[1, c].astype(F32)).astype(BF16)
        for c in (0, 1):
            last[c].wait_send()

    for r in range(4):
        @pl.when(away(r) != 0)
        def _():
            for c in (0, 1):
                x_copy(r, c, 1).wait_send()
    for c in sent:
        c.wait_send()
    assert ids[0] <= XBASE


VM = pl.BlockSpec(memory_space=pltpu.VMEM)
SM = pl.BlockSpec(memory_space=pltpu.SMEM)
HBM = pl.BlockSpec(memory_space=pltpu.HBM)
FREQ = (THETA ** (-2.0 * (np.arange(HD) % (HD // 2)) / HD)).astype(np.float32)[None]


def shards(store, owners, positions, sel_rows, sel_hidden, norm_gain, w_query, w_keyval, w_out):
    blended, mixed = pl.pallas_call(
        sublayer,
        name="sublayer",
        out_shape=(
            jax.ShapeDtypeStruct((L, HD), BF16),
            jax.ShapeDtypeStruct((SEL, 768), BF16),
        ),
        in_specs=[SM, SM, VM, VM, VM, HBM, HBM, HBM, HBM, HBM],
        out_specs=(VM, VM),
        scratch_shapes=[
            pltpu.VMEM((16, SEL, 768), BF16),
            pltpu.VMEM((768, 768), BF16),
            pltpu.VMEM((768, HD), BF16),
            pltpu.VMEM((768, 768), BF16),
            *[pltpu.VMEM((4, 4, n, HD), BF16) for _, n in PARTS],
            pltpu.VMEM((4, L, HD), BF16),
            pltpu.VMEM((4, L, HD), BF16),
            pltpu.VMEM((1, 4, SEL, PW), BF16),
            pltpu.VMEM((2, 2, SEL, PW), BF16),
            pltpu.VMEM((3, 4, SEL, PW), F32),
            pltpu.VMEM((2, 4, SEL, PW), BF16),
            pltpu.VMEM((2, 4, SEL, PW), BF16),
            pltpu.VMEM((4, SEL, PW), BF16),
            pltpu.VMEM((4, SEL, PW), BF16),
            pltpu.VMEM((4, 8, 128), F32),
            pltpu.VMEM((4, 8, 128), F32),
            pltpu.VMEM((8, 128), F32),
            pltpu.VMEM((4, 8, 128), F32),
            pltpu.VMEM((SEL, HD), F32),
            pltpu.VMEM((2, SEL + 8, HD), F32),
            pltpu.VMEM((2, 4, L, HD), BF16),
            pltpu.VMEM((2, 4, SEL, HD), BF16),
            pltpu.VMEM((4, L, HD), BF16),
            pltpu.VMEM((HD, 4 * L), BF16),
            pltpu.VMEM((2, L, HD), BF16),
            pltpu.VMEM((3, TQ, HD), BF16),
            pltpu.VMEM((4, L, TQ), F32),
            pltpu.VMEM((4, L, TQ), BF16),
            pltpu.VMEM((3, TQ, HD), BF16),
            pltpu.VMEM((3, 4, 8, 256), F32),
            pltpu.VMEM((3, 4, QC, HD), BF16),
            pltpu.VMEM((3, 4, 8, 256), F32),
            pltpu.VMEM((4, 4, SEL, 768), BF16),
            pltpu.VMEM((4, 2, 2, 2, SEL, OC), BF16),
            pltpu.VMEM((4, 2, 2, SEL, OC), BF16),
            pltpu.VMEM((4, 2, 2, SEL, OC), BF16),
            pltpu.VMEM((4, 2, SEL, OC), BF16),
            pltpu.VMEM((4, 2, SEL, OC), BF16),
            pltpu.VMEM((4, 2, SEL, OC), BF16),
            pltpu.VMEM((4, 2, 2, SEL, OC), BF16),
            pltpu.VMEM((2, SEL, OC), F32),
            pltpu.SemaphoreType.DMA((SEMS,)),
            pltpu.SemaphoreType.DMA((SEMS,)),
            pltpu.SemaphoreType.DMA((4 + NP,)),
        ],
        compiler_params=pltpu.CompilerParams(
            collective_id=0, has_side_effects=True, vmem_limit_bytes=60 * 2**20),
    )(owners, positions, sel_rows, norm_gain, jnp.asarray(FREQ),
      sel_hidden, w_query, w_keyval, store, w_out)
    return blended[None], mixed[None]


def solution(mesh):
    return jax.shard_map(
        shards,
        mesh=mesh,
        in_specs=(
            P("section", None, "tensor"),
            P(),
            P(),
            P(),
            P(None, None, "section"),
            P("section"),
            P("section", "tensor"),
            P("section", "tensor"),
            P("tensor", "section"),
        ),
        out_specs=(P("section", None, "tensor"), P("tensor", None, "section")),
        check_vma=False,
    )
```

```python
import math

import jax
import jax.numpy as jnp
import numpy as np
from jax import lax
from jax.experimental import pallas as pl
from jax.experimental.pallas import tpu as pltpu
from jax.sharding import PartitionSpec as P

D = 12288
HD = 128
HALF = 6
L = 640
SEL = 96
THETA = 1000000.0
EPS = 1e-05
MASKED = -1e30
MESH = pl.DeviceIdType.MESH
F32 = jnp.float32
BF16 = jnp.bfloat16
PW = 896
QN = HALF * SEL
QC = 2 * SEL
TQ = 4 * QC
PARTS = [(0, 192), (192, 256), (448, 192)]
NP = len(PARTS)
SCALE2 = math.log2(math.e) / math.sqrt(HD)
RC = SEL // 3
XBASE = 190
ORDER = (
    "s0", "a0", "s1", "m2", "f0", "m1", "f1", "r0", "s2", "r1", "m3", "f2", "m0", "F0",
    "t0", "F1", "q0", "F2", "r2", "t1", "N0", "N1", "o0", "Z0", "o1", "t2", "F3", "Z1",
    "E0", "N2", "p0", "o2", "p1", "N3", "Z2", "G0", "p2", "Q0", "Z3", "P0", "Q1", "A0",
    "Q2", "A1", "M0", "A2", "M1", "H0", "I0", "M2", "R00", "H1", "X00", "I1", "R01", "K0",
    "R30", "X01", "X30", "R10", "I2", "H2", "R02", "X10", "K1", "R31", "X02", "R11", "R20", "X31",
    "X20", "X11", "K2", "R12", "R21", "R32", "X12", "X21", "R22", "X32", "X22", "D1", "D0", "D2",
    "C0", "C1", "C2",
)
SEMS = 210


def spread(vec, lanes):
    return lax.dot_general(
        vec, jnp.ones((8, lanes), F32), (((0,), (0,)), ((), ())),
        precision=lax.Precision.HIGHEST, preferred_element_type=F32,
    )


def turned(v, c, sn):
    return v * c + pltpu.roll(v, 64, 1) * sn


def sublayer(owners, positions, rows, gain, freq, h_any, wq_any, wkv_any, store, wo_any,
             blended, mixed,
             h, wq, wkv, wo, st0, st1, st2, stsend, strecv, p2, p2r, acc, psend, precv, zsend,
             zrecv, sqs, sqr, sqz, sqzr, scale, trig, kvc, fr, keys, vt, first_kv, q, sbuf, pbuf, o, lse,
             orecv, lrecv, ag, prod, crecv, csum, xrecv, zlsend, zlrecv, fin, ssem, rsem, lsem):
    s = lax.axis_index("section")
    t = lax.axis_index("tensor")
    y, z = s // 4, s % 4
    x, zl, core = t // 4, (t // 2) % 2, t % 2
    kind = t // 8
    values = kind == 1

    def ypeer(d):
        return {"section": ((y + d) % 4) * 4 + z}

    def zpeer(d):
        return {"section": y * 4 + (z + d) % 4}

    def xpeer(d):
        return {"tensor": ((x + d) % 4) * 4 + t % 4}

    twin = {"tensor": x * 4 + zl * 2 + 1 - core}
    pair = {"tensor": x * 4 + (1 - zl) * 2 + core}
    partner = xpeer(2)
    sent = []
    ids = [0]

    def push(src, dst, dev):
        i = ids[0]
        ids[0] += 1
        c = pltpu.make_async_remote_copy(
            src_ref=src, dst_ref=dst, send_sem=ssem.at[i], recv_sem=rsem.at[i],
            device_id=dev, device_id_type=MESH)
        c.start()
        sent.append(c)
        return c

    def waits(copies):
        for c in copies:
            c.wait_recv()

    st = [st0, st1, st2]
    local = []

    def fetch(src, dst):
        c = pltpu.make_async_copy(src, dst, lsem.at[len(local)])
        c.start()
        local.append(c)

    fetch(h_any, h)
    fetch(wq_any, wq)
    fetch(wkv_any, wkv)
    for k, (lo, n) in enumerate(PARTS):
        fetch(store.at[:, pl.ds(lo, n)], st[k].at[y])
    fetch(wo_any, wo)

    peers = [f(d) for f in (ypeer, zpeer, xpeer) for d in (1, 2, 3)] + [twin, pair]
    barrier = pltpu.get_barrier_semaphore()
    for peer in peers:
        pl.semaphore_signal(barrier, inc=1, device_id=peer, device_id_type=MESH)
    pl.semaphore_wait(barrier, len(peers))

    def send_store(k):
        src = store.at[:, pl.ds(*PARTS[k])]
        return [push(src, st[k].at[y], ypeer(1)), push(src, st[k].at[y], ypeer(3))]

    def forward_store(k, copies):
        waits(copies)
        below, above = (y + 3) % 4, (y + 1) % 4
        a, b = st[k].at[below, pl.ds(0, 2)], st[k].at[above, pl.ds(2, 2)]
        return [push(a, a, ypeer(1)), push(b, b, ypeer(3))]

    def picked(k, d):
        slot = owners[y * 4 + (z + d) % 4]
        here = ((slot >> 2) & 3) == z
        block = st[k][slot >> 4, slot & 3]
        return jnp.where(here, block, jnp.zeros_like(block))

    def route_store(k, copies):
        local[3 + k].wait()
        waits(copies)
        part = pl.ds(*PARTS[k])
        out = []
        for d in (1, 3, 2):
            stsend[d, part] = picked(k, d)
            out.append(push(stsend.at[d, part], strecv.at[4 - d, part], zpeer(d)))
        return out

    ones8 = jnp.ones((8, 128), F32)
    gains = gain[...].astype(F32).reshape(1, 768)

    def multiply(d, out, i):
        hf = h[pl.ds(((y + d) % 4) * 4, 4)].astype(F32).reshape(4 * SEL, 768)
        hg = (hf * gains).astype(BF16)
        a = jnp.dot(hg, wkv[...], preferred_element_type=F32)
        b = jnp.dot(hg, wq[...], preferred_element_type=F32)
        out[i, :, :, :HD] = a.reshape(4, SEL, HD).astype(out.dtype)
        out[i, :, :, HD:] = b.reshape(4, SEL, 768).astype(out.dtype)
        sq = hf * hf
        part = sq[:, :128]
        for k in range(1, 6):
            part = part + sq[:, k * 128:(k + 1) * 128]
        sqs[d] = jnp.zeros((8, 128), F32)
        for g in range(4):
            row = lax.dot_general(
                ones8, part[g * SEL:(g + 1) * SEL], (((1,), (1,)), ((), ())),
                precision=lax.Precision.HIGHEST, preferred_element_type=F32)
            sqs[d, g:g + 1, :SEL] = row[:1]

    up2, dn2, up1, dn1 = {}, {}, {}, {}

    def chunk(k):
        if k == 0:
            return pl.ds(0, SEL), pl.ds(0, HD)
        return pl.ds((k - 1) * RC, RC), pl.ds(HD, 768)

    def send_far(k):
        at = chunk(k)
        up2[k] = push(p2.at[0, pl.ds(0, 2), *at], p2r.at[0, :, *at], ypeer(1))
        dn2[k] = push(p2.at[0, pl.ds(2, 2), *at], p2r.at[1, :, *at], ypeer(3))

    def send_near(k):
        at = chunk(k)
        up2[k].wait_recv()
        psend[0, :2, *at] = (acc[1, :2, *at] + p2r[0, :, *at].astype(F32)).astype(BF16)
        psend[0, 2:, *at] = acc[1, 2:, *at].astype(BF16)
        up1[k] = push(psend.at[0, :, *at], precv.at[0, :, *at], ypeer(1))
        dn2[k].wait_recv()
        psend[1, 2:, *at] = (acc[2, 2:, *at] + p2r[1, :, *at].astype(F32)).astype(BF16)
        psend[1, :2, *at] = acc[2, :2, *at].astype(BF16)
        dn1[k] = push(psend.at[1, :, *at], precv.at[1, :, *at], ypeer(3))

    total = acc.at[0]

    def send_z(k):
        at = chunk(k)
        up1[k].wait_recv()
        dn1[k].wait_recv()
        out = []
        for d in (1, 3, 2):
            g = (z + d) % 4
            zsend[d, *at] = (total[g, *at] + precv[0, g, *at].astype(F32)
                             + precv[1, g, *at].astype(F32)).astype(BF16)
            out.append(push(zsend.at[d, *at], zrecv.at[4 - d, *at], zpeer(d)))
        return out

    def settle(k, copies):
        cached = picked(k, 0)
        waits(copies)
        part = pl.ds(*PARTS[k])
        for d in (1, 2, 3):
            cached = cached + strecv[d, part]
        kvc[kind, 0, part] = turned(
            cached.astype(F32), trig[0, SEL:SEL + 1], trig[1, SEL:SEL + 1]).astype(BF16)
        mine = kvc.at[kind, 0, part]
        out = {4 - d: push(mine, kvc.at[kind, 4 - d, part], zpeer(d)) for d in (1, 3)}
        return out, [push(mine, mine, partner)]

    def pass_on(k, kz, kx):
        lo, n = PARTS[k]
        part = pl.ds(lo, n)
        for r, half, to in ((1, lo, 3), (3, lo + n // 2, 1)):
            kz[r].wait_recv()
            half = pl.ds(half, n // 2)
            kz[r + 4] = push(kvc.at[kind, r, half], kvc.at[kind, 2, half], zpeer(to))
            kx.append(push(kvc.at[kind, r, part], kvc.at[kind, r, part], partner))

    def pass_far(k, kz, kx):
        part = pl.ds(*PARTS[k])
        kz[5].wait_recv()
        kz[7].wait_recv()
        kx.append(push(kvc.at[kind, 2, part], kvc.at[kind, 2, part], partner))

    row8 = lax.broadcasted_iota(jnp.int32, (8, SEL), 0) == 0
    start = positions[s].astype(F32)
    my_rows = rows[pl.ds(s, 1), :].astype(F32)

    def angles():
        angle = spread(jnp.where(row8, my_rows + start, 0.0), HD) * freq[...]
        lane_sign = jnp.where(lax.broadcasted_iota(jnp.int32, (1, HD), 1) < 64, -1.0, 1.0)
        trig[0, :SEL] = jnp.cos(angle)
        trig[1, :SEL] = jnp.sin(angle) * lane_sign
        shift = jnp.broadcast_to(freq[...] * start, (8, HD))
        trig[0, SEL:] = jnp.where(values, 1.0, jnp.cos(shift))
        trig[1, SEL:] = jnp.where(values, 0.0, jnp.sin(shift) * lane_sign)

    sends, fars, routes, kz, kx, pz, qy = {}, {}, {}, {}, {}, {}, {}
    sq_y, sq_z, fz, fx = [], [], {}, []

    def do_send(k):
        sends[k] = send_store(k)

    def do_forward(k):
        fars[k] = forward_store(k, sends[k])

    def do_route(k):
        routes[k] = route_store(k, fars[k])

    def do_settle(k):
        kz[k], kx[k] = settle(k, routes[k])

    def do_multiply(d):
        if d == 2:
            for c in local[:3]:
                c.wait()
            multiply(2, p2, 0)
        else:
            multiply(d, acc, {1: 1, 3: 2, 0: 0}[d])
        if d:
            sq_y.append(push(sqs.at[d], sqr.at[4 - d], ypeer(d)))

    def do_z(k):
        pz[k] = send_z(k)

    def do_squares(_):
        waits(sq_y)
        sqz[...] = sqs[0] + sqr[1] + sqr[2] + sqr[3]
        sq_z.extend(push(sqz, sqzr.at[4 - d], zpeer(d)) for d in (1, 3, 2))

    def factor():
        waits(sq_z)
        squares = sqz[...] + sqzr[1] + sqzr[2] + sqzr[3]
        own = lax.broadcasted_iota(jnp.int32, (8, 128), 0) == z
        return lax.rsqrt(spread(jnp.where(own, squares, 0.0), HD)[:SEL] / D + EPS)

    def summed(at):
        v = total[z, *at] + precv[0, z, *at].astype(F32) + precv[1, z, *at].astype(F32)
        for d in (1, 2, 3):
            v = v + zrecv[d, *at].astype(F32)
        return v * scale[at[0]]

    def do_fresh(_):
        scale[...] = factor()
        waits(pz[0])
        fr[kind, 0] = turned(
            summed(chunk(0)), jnp.where(values, 1.0, trig[0, :SEL]),
            jnp.where(values, 0.0, trig[1, :SEL])).astype(BF16)
        for d in (1, 3, 2):
            fz[4 - d] = push(fr.at[kind, 0], fr.at[kind, 4 - d], zpeer(d))
        fx.append(push(fr.at[kind, 0], fr.at[kind, 0], partner))

    def do_fresh_over(_):
        for r in (3, 1, 2):
            fz[r].wait_recv()
            fx.append(push(fr.at[kind, r], fr.at[kind, r], partner))

    def send_queries(k):
        waits(pz[k + 1])
        lines = pl.ds(k * RC, RC)
        for j in range(HALF):
            q[k, j * RC:(j + 1) * RC] = turned(
                summed((lines, pl.ds(HD + j * HD, HD))),
                trig[0, lines], trig[1, lines]).astype(BF16)
        mine = q.at[k, pl.ds(0, QC)]
        qy[k] = [push(mine, q.at[k, pl.ds((4 - d) * QC, QC)], ypeer(d)) for d in (1, 3, 2)]

    def do_patch(_):
        for copies in kx.values():
            waits(copies)
        waits(fx)
        for r in range(4):
            group = rows[pl.ds(y * 4 + (z + r) % 4, 1), :]
            hit = lax.broadcasted_iota(jnp.int32, (L, SEL), 0) == group
            hot = jnp.where(hit, 1.0, 0.0)
            taken = jnp.max(hot, axis=1, keepdims=True) > 0.0
            hot = hot.astype(BF16)
            for k in (0, 1):
                placed = jnp.dot(hot, fr[k, r], preferred_element_type=F32)
                patched = jnp.where(taken, placed, kvc[k, r].astype(F32))
                if r == 0:
                    first_kv[k] = patched.astype(BF16)
                if k == 0:
                    keys[r] = patched.astype(BF16)
                else:
                    vt[:, r * L:(r + 1) * L] = patched.T.astype(BF16)
        blended[...] = first_kv[kind]

    lane = lax.broadcasted_iota(jnp.int32, (1, TQ), 1)
    first = jnp.full((1, TQ), positions[y * 4 + z], jnp.int32)
    for d in (1, 2, 3):
        first = jnp.where(lane >= d * QC, positions[((y + d) % 4) * 4 + z], first)

    def limits(k):
        tiled = (lax.broadcasted_iota(jnp.int32, (SEL, TQ), 1) % RC + k * RC
                 == lax.broadcasted_iota(jnp.int32, (SEL, TQ), 0))
        limit = lax.dot_general(
            jnp.where(row8, my_rows, 0.0), jnp.where(tiled, 1.0, 0.0), (((1,), (0,)), ((), ())),
            precision=lax.Precision.HIGHEST, preferred_element_type=F32)[:1]
        return jnp.where(lane < QC, limit, float(L))

    hidden = [positions[y * 4 + (z + e) % 4] > first for e in range(4)]

    def attend(k):
        waits(qy[k])
        limit = limits(k)
        block = q[k]
        top = jnp.full((1, TQ), MASKED, F32)
        for e in range(4):
            sc = lax.dot_general(
                keys[e], block, (((1,), (1,)), ((), ())), preferred_element_type=F32)
            if e == 0:
                line = lax.broadcasted_iota(jnp.int32, (L, TQ), 0).astype(F32)
                sc = jnp.where(line <= limit, sc, MASKED)
            sbuf[e] = sc
            top = jnp.maximum(
                top, jnp.where(hidden[e], MASKED, jnp.max(sc, axis=0, keepdims=True)))
        top = top * SCALE2
        weight = jnp.zeros((1, TQ), F32)
        for e in range(4):
            base = top + jnp.where(hidden[e], 1e30, 0.0)
            p = jnp.exp2(sbuf[e] * SCALE2 - base)
            weight = weight + jnp.sum(p, axis=0, keepdims=True)
            pbuf[e] = p.astype(BF16)
        num = jnp.dot(vt[...], pbuf[...].reshape(4 * L, TQ), preferred_element_type=F32)
        some = weight > 0.0
        safe = jnp.where(some, weight, 1.0)
        o[k] = (num * (1.0 / safe)).T.astype(BF16)
        logs = jnp.broadcast_to(jnp.where(some, top + jnp.log2(safe), MASKED), (8, TQ))
        for d in range(4):
            moved = pltpu.roll(logs, TQ - d * QC, 1) if d else logs
            lse[k, d] = moved[:, :256]
        got = {}
        for d in (2, 1, 3):
            got[4 - d] = [push(o.at[k, pl.ds(d * QC, QC)], orecv.at[k, 4 - d], ypeer(d)),
                          push(lse.at[k, d], lrecv.at[k, 4 - d], ypeer(d))]
        return got

    def merge(k, got):
        for r in (1, 3, 2):
            waits(got[r])
        logs = [lse[k, 0, :1]] + [lrecv[k, r, :1] for r in (1, 2, 3)]
        top = jnp.maximum(jnp.maximum(logs[0], logs[1]), jnp.maximum(logs[2], logs[3]))
        share = [jnp.exp2(v - top) for v in logs]
        whole = share[0] + share[1] + share[2] + share[3]
        line = lax.broadcasted_iota(jnp.int32, (8, 256), 0) == 0
        merged = jnp.zeros((QC, HD), F32)
        for r in range(4):
            part = o[k, :QC] if r == 0 else orecv[k, r]
            col = spread(jnp.where(line, share[r] / whole, 0.0), HD)[:QC]
            merged = merged + part.astype(F32) * col
        for j in range(HALF):
            ag[0, z, k * RC:(k + 1) * RC, j * HD:(j + 1) * HD] = (
                merged[j * RC:(j + 1) * RC].astype(BF16))

    zs, ups, dns, fw = {}, {}, {}, {}

    def block_of(r, k, d):
        return ag.at[r, (z + d) % 4, pl.ds(k * RC, RC)]

    def send_y(k, d):
        ups[k, d] = push(block_of(0, k, d), block_of(3, k, d), ypeer(1))
        dns[k, d] = push(block_of(0, k, d), block_of(1, k, d), ypeer(3))

    def gather_start(k, got):
        merge(k, got)
        mine = block_of(0, k, 0)
        zs[k, 1] = push(mine, mine, zpeer(1))
        zs[k, 3] = push(mine, mine, zpeer(3))
        send_y(k, 0)
        zs[k, 2] = push(mine, mine, zpeer(2))

    def gather_z(k, blocks):
        for d in blocks:
            zs[k, 4 - d].wait_recv()
            send_y(k, d)

    def gather_far(k):
        for d in (0, 3, 1, 2):
            ups[k, d].wait_recv()
            dns[k, d].wait_recv()
            if d in (0, 3):
                fw[k, d] = push(block_of(3, k, d), block_of(2, k, d), ypeer(1))
            else:
                fw[k, d] = push(block_of(1, k, d), block_of(2, k, d), ypeer(3))

    def x_copy(r, k, slot):
        return pltpu.make_async_remote_copy(
            src_ref=csum.at[r, k], dst_ref=xrecv.at[slot, k], send_sem=ssem.at[XBASE + 3 * r + k],
            recv_sem=rsem.at[XBASE + 3 * slot + k], device_id=xpeer(4 - slot),
            device_id_type=MESH)

    def away(r):
        return (y + r + 4 - x) % 4

    home = (x + 4 - y) % 4

    parts, tw = {}, {}

    def do_product(r, k):
        if not tw:
            local[3 + NP].wait()
        if r == 2:
            for d in (0, 3, 1, 2):
                fw[k, d].wait_recv()
        a = jnp.dot(ag[r, :, k * RC:(k + 1) * RC].reshape(4 * RC, 768), wo[...],
                    preferred_element_type=F32).reshape(4, RC, 768).astype(BF16)
        for g in range(4):
            prod[r, k, g % 2, g // 2] = a[g]
        tw[r, k] = push(prod.at[r, k, 1 - core], crecv.at[r, k], twin)

    def do_x(r, k):
        tw[r, k].wait_recv()
        csum[r, k] = (prod[r, k, core].astype(F32) + crecv[r, k].astype(F32)).astype(BF16)

        @pl.when(away(r) != 0)
        def _():
            x_copy(r, k, (4 - away(r)) % 4).start()

    last = {}

    def do_pair(k):
        for slot in (1, 2, 3):
            x_copy(0, k, slot).wait_recv()

        def over_x(half):
            v = csum[home, k, half].astype(F32)
            for slot in (1, 2, 3):
                v = v + xrecv[slot, k, half].astype(F32)
            return v

        zlsend[k] = over_x(1 - zl).astype(BF16)
        last[k] = push(zlsend.at[k], zlrecv.at[k], pair)
        fin[k] = over_x(zl)

    def do_close(k):
        last[k].wait_recv()
        mixed[k * RC:(k + 1) * RC] = (fin[k] + zlrecv[k].astype(F32)).astype(BF16)

    def do_attend(k):
        parts[k] = attend(k)

    steps = {
        "s": do_send, "f": do_forward, "r": do_route, "t": do_settle,
        "o": lambda k: pass_on(k, kz[k], kx[k]), "p": lambda k: pass_far(k, kz[k], kx[k]),
        "m": do_multiply, "F": send_far, "N": send_near, "Z": do_z, "a": lambda _: angles(),
        "q": do_squares, "E": do_fresh, "G": do_fresh_over, "Q": send_queries, "P": do_patch,
        "A": do_attend, "M": lambda k: gather_start(k, parts[k]),
        "H": lambda k: gather_z(k, (3, 1)), "I": lambda k: gather_z(k, (2,)), "K": gather_far,
        "R": do_product, "X": do_x, "D": do_pair, "C": do_close,
    }
    for step in ORDER:
        steps[step[0]](*[int(n) for n in step[1:]])
    for r in range(4):
        @pl.when(away(r) != 0)
        def _():
            for k in range(3):
                x_copy(r, k, 1).wait_send()
    for c in sent:
        c.wait_send()
    assert ids[0] <= XBASE


VM = pl.BlockSpec(memory_space=pltpu.VMEM)
SM = pl.BlockSpec(memory_space=pltpu.SMEM)
HBM = pl.BlockSpec(memory_space=pltpu.HBM)
FREQ = (THETA ** (-2.0 * (np.arange(HD) % (HD // 2)) / HD)).astype(np.float32)[None]


def shards(store, owners, positions, sel_rows, sel_hidden, norm_gain, w_query, w_keyval, w_out):
    blended, mixed = pl.pallas_call(
        sublayer,
        name="sublayer",
        out_shape=(
            jax.ShapeDtypeStruct((L, HD), BF16),
            jax.ShapeDtypeStruct((SEL, 768), BF16),
        ),
        in_specs=[SM, SM, VM, VM, VM, HBM, HBM, HBM, HBM, HBM],
        out_specs=(VM, VM),
        scratch_shapes=[
            pltpu.VMEM((16, SEL, 768), BF16),
            pltpu.VMEM((768, 768), BF16),
            pltpu.VMEM((768, HD), BF16),
            pltpu.VMEM((768, 768), BF16),
            *[pltpu.VMEM((4, 4, n, HD), BF16) for _, n in PARTS],
            pltpu.VMEM((4, L, HD), BF16),
            pltpu.VMEM((4, L, HD), BF16),
            pltpu.VMEM((1, 4, SEL, PW), BF16),
            pltpu.VMEM((2, 2, SEL, PW), BF16),
            pltpu.VMEM((3, 4, SEL, PW), F32),
            pltpu.VMEM((2, 4, SEL, PW), BF16),
            pltpu.VMEM((2, 4, SEL, PW), BF16),
            pltpu.VMEM((4, SEL, PW), BF16),
            pltpu.VMEM((4, SEL, PW), BF16),
            pltpu.VMEM((4, 8, 128), F32),
            pltpu.VMEM((4, 8, 128), F32),
            pltpu.VMEM((8, 128), F32),
            pltpu.VMEM((4, 8, 128), F32),
            pltpu.VMEM((SEL, HD), F32),
            pltpu.VMEM((2, SEL + 8, HD), F32),
            pltpu.VMEM((2, 4, L, HD), BF16),
            pltpu.VMEM((2, 4, SEL, HD), BF16),
            pltpu.VMEM((4, L, HD), BF16),
            pltpu.VMEM((HD, 4 * L), BF16),
            pltpu.VMEM((2, L, HD), BF16),
            pltpu.VMEM((3, TQ, HD), BF16),
            pltpu.VMEM((4, L, TQ), F32),
            pltpu.VMEM((4, L, TQ), BF16),
            pltpu.VMEM((3, TQ, HD), BF16),
            pltpu.VMEM((3, 4, 8, 256), F32),
            pltpu.VMEM((3, 4, QC, HD), BF16),
            pltpu.VMEM((3, 4, 8, 256), F32),
            pltpu.VMEM((4, 4, SEL, 768), BF16),
            pltpu.VMEM((4, 3, 2, 2, RC, 768), BF16),
            pltpu.VMEM((4, 3, 2, RC, 768), BF16),
            pltpu.VMEM((4, 3, 2, RC, 768), BF16),
            pltpu.VMEM((4, 3, 2, RC, 768), BF16),
            pltpu.VMEM((3, RC, 768), BF16),
            pltpu.VMEM((3, RC, 768), BF16),
            pltpu.VMEM((3, RC, 768), F32),
            pltpu.SemaphoreType.DMA((SEMS,)),
            pltpu.SemaphoreType.DMA((SEMS,)),
            pltpu.SemaphoreType.DMA((4 + NP,)),
        ],
        compiler_params=pltpu.CompilerParams(
            collective_id=0, has_side_effects=True, vmem_limit_bytes=60 * 2**20),
    )(owners, positions, sel_rows, norm_gain, jnp.asarray(FREQ),
      sel_hidden, w_query, w_keyval, store, w_out)
    return blended[None], mixed[None]


def solution(mesh):
    return jax.shard_map(
        shards,
        mesh=mesh,
        in_specs=(
            P("section", None, "tensor"),
            P(),
            P(),
            P(),
            P(None, None, "section"),
            P("section"),
            P("section", "tensor"),
            P("section", "tensor"),
            P("tensor", "section"),
        ),
        out_specs=(P("section", None, "tensor"), P("tensor", None, "section")),
        check_vma=False,
    )
```

```python
import math

import jax
import jax.numpy as jnp
import numpy as np
from jax import lax
from jax.experimental import pallas as pl
from jax.experimental.pallas import tpu as pltpu
from jax.sharding import PartitionSpec as P

D = 12288
HD = 128
HALF = 6
L = 640
SEL = 96
THETA = 1000000.0
EPS = 1e-05
MASKED = -1e30
MESH = pl.DeviceIdType.MESH
F32 = jnp.float32
BF16 = jnp.bfloat16
PW = 896
QN = HALF * SEL
QC = 2 * SEL
TQ = 4 * QC
PARTS = [(0, 192), (192, 256), (448, 192)]
NP = len(PARTS)
SCALE2 = math.log2(math.e) / math.sqrt(HD)
RC = SEL // 3
XBASE = 190
ORDER = (
    "s0", "a0", "s1", "m2", "f0", "m1", "f1", "r0", "s2", "r1", "m3", "f2", "m0", "B0",
    "F0", "t0", "F1", "q0", "F2", "r2", "t1", "N0", "N1", "o0", "Z0", "o1", "t2", "F3",
    "Z1", "E0", "N2", "p0", "o2", "p1", "N3", "Z2", "P0", "G0", "p2", "Q0", "Z3", "P1",
    "P3", "P2", "Q1", "A0", "Q2", "A1", "M0", "A2", "M1", "H0", "I0", "M2", "R00", "H1",
    "X00", "I1", "R01", "K0", "R30", "X01", "X30", "R10", "I2", "H2", "R02", "X10", "K1", "R31",
    "X02", "R11", "R20", "X31", "X20", "X11", "K2", "R12", "R21", "R32", "X12", "X21", "R22", "X32",
    "X22", "D1", "D0", "D2", "C0", "C1", "C2",
)
SEMS = 210


def spread(vec, lanes):
    return lax.dot_general(
        vec, jnp.ones((8, lanes), F32), (((0,), (0,)), ((), ())),
        precision=lax.Precision.HIGHEST, preferred_element_type=F32,
    )


def turned(v, c, sn):
    return v * c + pltpu.roll(v, 64, 1) * sn


def sublayer(owners, positions, rows, gain, freq, h_any, wq_any, wkv_any, store, wo_any,
             blended, mixed,
             h, wq, wkv, wo, st0, st1, st2, stsend, strecv, p2, p2r, acc, psend, precv, zsend,
             zrecv, sqs, sqr, sqz, sqzr, scale, trig, kvc, fr, hots, taken, lim, keys, vt, first_kv, q, sbuf, pbuf, o, lse,
             orecv, lrecv, ag, prod, crecv, csum, xrecv, zlsend, zlrecv, fin, ssem, rsem, lsem):
    s = lax.axis_index("section")
    t = lax.axis_index("tensor")
    y, z = s // 4, s % 4
    x, zl, core = t // 4, (t // 2) % 2, t % 2
    kind = t // 8
    values = kind == 1

    def ypeer(d):
        return {"section": ((y + d) % 4) * 4 + z}

    def zpeer(d):
        return {"section": y * 4 + (z + d) % 4}

    def xpeer(d):
        return {"tensor": ((x + d) % 4) * 4 + t % 4}

    twin = {"tensor": x * 4 + zl * 2 + 1 - core}
    pair = {"tensor": x * 4 + (1 - zl) * 2 + core}
    partner = xpeer(2)
    sent = []
    ids = [0]

    def push(src, dst, dev):
        i = ids[0]
        ids[0] += 1
        c = pltpu.make_async_remote_copy(
            src_ref=src, dst_ref=dst, send_sem=ssem.at[i], recv_sem=rsem.at[i],
            device_id=dev, device_id_type=MESH)
        c.start()
        sent.append(c)
        return c

    def waits(copies):
        for c in copies:
            c.wait_recv()

    st = [st0, st1, st2]
    local = []

    def fetch(src, dst):
        c = pltpu.make_async_copy(src, dst, lsem.at[len(local)])
        c.start()
        local.append(c)

    fetch(h_any, h)
    fetch(wq_any, wq)
    fetch(wkv_any, wkv)
    for k, (lo, n) in enumerate(PARTS):
        fetch(store.at[:, pl.ds(lo, n)], st[k].at[y])
    fetch(wo_any, wo)

    peers = [f(d) for f in (ypeer, zpeer, xpeer) for d in (1, 2, 3)] + [twin, pair]
    barrier = pltpu.get_barrier_semaphore()
    for peer in peers:
        pl.semaphore_signal(barrier, inc=1, device_id=peer, device_id_type=MESH)
    pl.semaphore_wait(barrier, len(peers))

    def send_store(k):
        src = store.at[:, pl.ds(*PARTS[k])]
        return [push(src, st[k].at[y], ypeer(1)), push(src, st[k].at[y], ypeer(3))]

    def forward_store(k, copies):
        waits(copies)
        below, above = (y + 3) % 4, (y + 1) % 4
        a, b = st[k].at[below, pl.ds(0, 2)], st[k].at[above, pl.ds(2, 2)]
        return [push(a, a, ypeer(1)), push(b, b, ypeer(3))]

    def picked(k, d):
        slot = owners[y * 4 + (z + d) % 4]
        here = ((slot >> 2) & 3) == z
        block = st[k][slot >> 4, slot & 3]
        return jnp.where(here, block, jnp.zeros_like(block))

    def route_store(k, copies):
        local[3 + k].wait()
        waits(copies)
        part = pl.ds(*PARTS[k])
        out = []
        for d in (1, 3, 2):
            stsend[d, part] = picked(k, d)
            out.append(push(stsend.at[d, part], strecv.at[4 - d, part], zpeer(d)))
        return out

    ones8 = jnp.ones((8, 128), F32)
    gains = gain[...].astype(F32).reshape(1, 768)

    def multiply(d, out, i):
        hf = h[pl.ds(((y + d) % 4) * 4, 4)].astype(F32).reshape(4 * SEL, 768)
        hg = (hf * gains).astype(BF16)
        a = jnp.dot(hg, wkv[...], preferred_element_type=F32)
        b = jnp.dot(hg, wq[...], preferred_element_type=F32)
        out[i, :, :, :HD] = a.reshape(4, SEL, HD).astype(out.dtype)
        out[i, :, :, HD:] = b.reshape(4, SEL, 768).astype(out.dtype)
        sq = hf * hf
        part = sq[:, :128]
        for k in range(1, 6):
            part = part + sq[:, k * 128:(k + 1) * 128]
        sqs[d] = jnp.zeros((8, 128), F32)
        for g in range(4):
            row = lax.dot_general(
                ones8, part[g * SEL:(g + 1) * SEL], (((1,), (1,)), ((), ())),
                precision=lax.Precision.HIGHEST, preferred_element_type=F32)
            sqs[d, g:g + 1, :SEL] = row[:1]

    up2, dn2, up1, dn1 = {}, {}, {}, {}

    def chunk(k):
        if k == 0:
            return pl.ds(0, SEL), pl.ds(0, HD)
        return pl.ds((k - 1) * RC, RC), pl.ds(HD, 768)

    def send_far(k):
        at = chunk(k)
        up2[k] = push(p2.at[0, pl.ds(0, 2), *at], p2r.at[0, :, *at], ypeer(1))
        dn2[k] = push(p2.at[0, pl.ds(2, 2), *at], p2r.at[1, :, *at], ypeer(3))

    def send_near(k):
        at = chunk(k)
        up2[k].wait_recv()
        psend[0, :2, *at] = (acc[1, :2, *at] + p2r[0, :, *at].astype(F32)).astype(BF16)
        psend[0, 2:, *at] = acc[1, 2:, *at].astype(BF16)
        up1[k] = push(psend.at[0, :, *at], precv.at[0, :, *at], ypeer(1))
        dn2[k].wait_recv()
        psend[1, 2:, *at] = (acc[2, 2:, *at] + p2r[1, :, *at].astype(F32)).astype(BF16)
        psend[1, :2, *at] = acc[2, :2, *at].astype(BF16)
        dn1[k] = push(psend.at[1, :, *at], precv.at[1, :, *at], ypeer(3))

    total = acc.at[0]

    def send_z(k):
        at = chunk(k)
        up1[k].wait_recv()
        dn1[k].wait_recv()
        out = []
        for d in (1, 3, 2):
            g = (z + d) % 4
            zsend[d, *at] = (total[g, *at] + precv[0, g, *at].astype(F32)
                             + precv[1, g, *at].astype(F32)).astype(BF16)
            out.append(push(zsend.at[d, *at], zrecv.at[4 - d, *at], zpeer(d)))
        return out

    def settle(k, copies):
        cached = picked(k, 0)
        waits(copies)
        part = pl.ds(*PARTS[k])
        for d in (1, 2, 3):
            cached = cached + strecv[d, part]
        kvc[kind, 0, part] = turned(
            cached.astype(F32), trig[0, SEL:SEL + 1], trig[1, SEL:SEL + 1]).astype(BF16)
        mine = kvc.at[kind, 0, part]
        out = {4 - d: push(mine, kvc.at[kind, 4 - d, part], zpeer(d)) for d in (1, 3)}
        return out, [push(mine, mine, partner)]

    def pass_on(k, kz, kx):
        lo, n = PARTS[k]
        part = pl.ds(lo, n)
        for r, half, to in ((1, lo, 3), (3, lo + n // 2, 1)):
            kz[r].wait_recv()
            half = pl.ds(half, n // 2)
            kz[r + 4] = push(kvc.at[kind, r, half], kvc.at[kind, 2, half], zpeer(to))
            kx.append(push(kvc.at[kind, r, part], kvc.at[kind, r, part], partner))

    def pass_far(k, kz, kx):
        part = pl.ds(*PARTS[k])
        kz[5].wait_recv()
        kz[7].wait_recv()
        kx.append(push(kvc.at[kind, 2, part], kvc.at[kind, 2, part], partner))

    row8 = lax.broadcasted_iota(jnp.int32, (8, SEL), 0) == 0
    start = positions[s].astype(F32)
    my_rows = rows[pl.ds(s, 1), :].astype(F32)

    def angles():
        angle = spread(jnp.where(row8, my_rows + start, 0.0), HD) * freq[...]
        lane_sign = jnp.where(lax.broadcasted_iota(jnp.int32, (1, HD), 1) < 64, -1.0, 1.0)
        trig[0, :SEL] = jnp.cos(angle)
        trig[1, :SEL] = jnp.sin(angle) * lane_sign
        shift = jnp.broadcast_to(freq[...] * start, (8, HD))
        trig[0, SEL:] = jnp.where(values, 1.0, jnp.cos(shift))
        trig[1, SEL:] = jnp.where(values, 0.0, jnp.sin(shift) * lane_sign)

    sends, fars, routes, kz, kx, pz, qy = {}, {}, {}, {}, {}, {}, {}
    sq_y, sq_z, fz, fx = [], [], {}, []

    def do_send(k):
        sends[k] = send_store(k)

    def do_forward(k):
        fars[k] = forward_store(k, sends[k])

    def do_route(k):
        routes[k] = route_store(k, fars[k])

    def do_settle(k):
        kz[k], kx[k] = settle(k, routes[k])

    def do_multiply(d):
        if d == 2:
            for c in local[:3]:
                c.wait()
            multiply(2, p2, 0)
        else:
            multiply(d, acc, {1: 1, 3: 2, 0: 0}[d])
        if d:
            sq_y.append(push(sqs.at[d], sqr.at[4 - d], ypeer(d)))

    def do_z(k):
        pz[k] = send_z(k)

    def do_squares(_):
        waits(sq_y)
        sqz[...] = sqs[0] + sqr[1] + sqr[2] + sqr[3]
        sq_z.extend(push(sqz, sqzr.at[4 - d], zpeer(d)) for d in (1, 3, 2))

    def factor():
        waits(sq_z)
        squares = sqz[...] + sqzr[1] + sqzr[2] + sqzr[3]
        own = lax.broadcasted_iota(jnp.int32, (8, 128), 0) == z
        return lax.rsqrt(spread(jnp.where(own, squares, 0.0), HD)[:SEL] / D + EPS)

    def summed(at):
        v = total[z, *at] + precv[0, z, *at].astype(F32) + precv[1, z, *at].astype(F32)
        for d in (1, 2, 3):
            v = v + zrecv[d, *at].astype(F32)
        return v * scale[at[0]]

    def do_fresh(_):
        scale[...] = factor()
        waits(pz[0])
        fr[kind, 0] = turned(
            summed(chunk(0)), jnp.where(values, 1.0, trig[0, :SEL]),
            jnp.where(values, 0.0, trig[1, :SEL])).astype(BF16)
        for d in (1, 3, 2):
            fz[4 - d] = push(fr.at[kind, 0], fr.at[kind, 4 - d], zpeer(d))
        fx.append(push(fr.at[kind, 0], fr.at[kind, 0], partner))

    def do_fresh_over(_):
        for r in (3, 1, 2):
            fz[r].wait_recv()
            fx.append(push(fr.at[kind, r], fr.at[kind, r], partner))

    def send_queries(k):
        waits(pz[k + 1])
        lines = pl.ds(k * RC, RC)
        for j in range(HALF):
            q[k, j * RC:(j + 1) * RC] = turned(
                summed((lines, pl.ds(HD + j * HD, HD))),
                trig[0, lines], trig[1, lines]).astype(BF16)
        mine = q.at[k, pl.ds(0, QC)]
        qy[k] = [push(mine, q.at[k, pl.ds((4 - d) * QC, QC)], ypeer(d)) for d in (1, 3, 2)]

    def do_patch(r):
        place = {0: 0, 1: 1, 3: 2, 2: 3}[r]
        for copies in kx.values():
            copies[place].wait_recv()
        fx[{0: 0, 3: 1, 1: 2, 2: 3}[r]].wait_recv()
        for k in (0, 1):
            placed = jnp.dot(hots[r], fr[k, r], preferred_element_type=F32)
            patched = jnp.where(taken[r] > 0.0, placed, kvc[k, r].astype(F32))
            if r == 0:
                first_kv[k] = patched.astype(BF16)
            if k == 0:
                keys[r] = patched.astype(BF16)
            else:
                vt[:, r * L:(r + 1) * L] = patched.T.astype(BF16)
        if r == 0:
            blended[...] = first_kv[kind]

    def do_masks(_):
        for r in range(4):
            group = rows[pl.ds(y * 4 + (z + r) % 4, 1), :]
            hit = lax.broadcasted_iota(jnp.int32, (L, SEL), 0) == group
            hot = jnp.where(hit, 1.0, 0.0)
            hots[r] = hot.astype(BF16)
            taken[r] = jnp.broadcast_to(jnp.max(hot, axis=1, keepdims=True), (L, HD))
        for k in range(3):
            lim[k] = jnp.broadcast_to(limits(k), (8, TQ))

    lane = lax.broadcasted_iota(jnp.int32, (1, TQ), 1)
    first = jnp.full((1, TQ), positions[y * 4 + z], jnp.int32)
    for d in (1, 2, 3):
        first = jnp.where(lane >= d * QC, positions[((y + d) % 4) * 4 + z], first)

    def limits(k):
        tiled = (lax.broadcasted_iota(jnp.int32, (SEL, TQ), 1) % RC + k * RC
                 == lax.broadcasted_iota(jnp.int32, (SEL, TQ), 0))
        limit = lax.dot_general(
            jnp.where(row8, my_rows, 0.0), jnp.where(tiled, 1.0, 0.0), (((1,), (0,)), ((), ())),
            precision=lax.Precision.HIGHEST, preferred_element_type=F32)[:1]
        return jnp.where(lane < QC, limit, float(L))

    hidden = [positions[y * 4 + (z + e) % 4] > first for e in range(4)]

    def attend(k):
        waits(qy[k])
        limit = lim[k, :1]
        block = q[k]
        top = jnp.full((1, TQ), MASKED, F32)
        for e in range(4):
            sc = lax.dot_general(
                keys[e], block, (((1,), (1,)), ((), ())), preferred_element_type=F32)
            if e == 0:
                line = lax.broadcasted_iota(jnp.int32, (L, TQ), 0).astype(F32)
                sc = jnp.where(line <= limit, sc, MASKED)
            sbuf[e] = sc
            top = jnp.maximum(
                top, jnp.where(hidden[e], MASKED, jnp.max(sc, axis=0, keepdims=True)))
        top = top * SCALE2
        weight = jnp.zeros((1, TQ), F32)
        for e in range(4):
            base = top + jnp.where(hidden[e], 1e30, 0.0)
            p = jnp.exp2(sbuf[e] * SCALE2 - base)
            weight = weight + jnp.sum(p, axis=0, keepdims=True)
            pbuf[e] = p.astype(BF16)
        num = jnp.dot(vt[...], pbuf[...].reshape(4 * L, TQ), preferred_element_type=F32)
        some = weight > 0.0
        safe = jnp.where(some, weight, 1.0)
        o[k] = (num * (1.0 / safe)).T.astype(BF16)
        logs = jnp.broadcast_to(jnp.where(some, top + jnp.log2(safe), MASKED), (8, TQ))
        for d in range(4):
            moved = pltpu.roll(logs, TQ - d * QC, 1) if d else logs
            lse[k, d] = moved[:, :256]
        got = {}
        for d in (2, 1, 3):
            got[4 - d] = [push(o.at[k, pl.ds(d * QC, QC)], orecv.at[k, 4 - d], ypeer(d)),
                          push(lse.at[k, d], lrecv.at[k, 4 - d], ypeer(d))]
        return got

    def merge(k, got):
        for r in (1, 3, 2):
            waits(got[r])
        logs = [lse[k, 0, :1]] + [lrecv[k, r, :1] for r in (1, 2, 3)]
        top = jnp.maximum(jnp.maximum(logs[0], logs[1]), jnp.maximum(logs[2], logs[3]))
        share = [jnp.exp2(v - top) for v in logs]
        whole = share[0] + share[1] + share[2] + share[3]
        line = lax.broadcasted_iota(jnp.int32, (8, 256), 0) == 0
        merged = jnp.zeros((QC, HD), F32)
        for r in range(4):
            part = o[k, :QC] if r == 0 else orecv[k, r]
            col = spread(jnp.where(line, share[r] / whole, 0.0), HD)[:QC]
            merged = merged + part.astype(F32) * col
        for j in range(HALF):
            ag[0, z, k * RC:(k + 1) * RC, j * HD:(j + 1) * HD] = (
                merged[j * RC:(j + 1) * RC].astype(BF16))

    zs, ups, dns, fw = {}, {}, {}, {}

    def block_of(r, k, d):
        return ag.at[r, (z + d) % 4, pl.ds(k * RC, RC)]

    def send_y(k, d):
        ups[k, d] = push(block_of(0, k, d), block_of(3, k, d), ypeer(1))
        dns[k, d] = push(block_of(0, k, d), block_of(1, k, d), ypeer(3))

    def gather_start(k, got):
        merge(k, got)
        mine = block_of(0, k, 0)
        zs[k, 1] = push(mine, mine, zpeer(1))
        zs[k, 3] = push(mine, mine, zpeer(3))
        send_y(k, 0)
        zs[k, 2] = push(mine, mine, zpeer(2))

    def gather_z(k, blocks):
        for d in blocks:
            zs[k, 4 - d].wait_recv()
            send_y(k, d)

    def gather_far(k):
        for d in (0, 3, 1, 2):
            ups[k, d].wait_recv()
            dns[k, d].wait_recv()
            if d in (0, 3):
                fw[k, d] = push(block_of(3, k, d), block_of(2, k, d), ypeer(1))
            else:
                fw[k, d] = push(block_of(1, k, d), block_of(2, k, d), ypeer(3))

    def x_copy(r, k, slot):
        return pltpu.make_async_remote_copy(
            src_ref=csum.at[r, k], dst_ref=xrecv.at[slot, k], send_sem=ssem.at[XBASE + 3 * r + k],
            recv_sem=rsem.at[XBASE + 3 * slot + k], device_id=xpeer(4 - slot),
            device_id_type=MESH)

    def away(r):
        return (y + r + 4 - x) % 4

    home = (x + 4 - y) % 4

    parts, tw = {}, {}

    def do_product(r, k):
        if not tw:
            local[3 + NP].wait()
        if r == 2:
            for d in (0, 3, 1, 2):
                fw[k, d].wait_recv()
        a = jnp.dot(ag[r, :, k * RC:(k + 1) * RC].reshape(4 * RC, 768), wo[...],
                    preferred_element_type=F32).reshape(4, RC, 768).astype(BF16)
        for g in range(4):
            prod[r, k, g % 2, g // 2] = a[g]
        tw[r, k] = push(prod.at[r, k, 1 - core], crecv.at[r, k], twin)

    def do_x(r, k):
        tw[r, k].wait_recv()
        csum[r, k] = (prod[r, k, core].astype(F32) + crecv[r, k].astype(F32)).astype(BF16)

        @pl.when(away(r) != 0)
        def _():
            x_copy(r, k, (4 - away(r)) % 4).start()

    last = {}

    def do_pair(k):
        for slot in (1, 2, 3):
            x_copy(0, k, slot).wait_recv()

        def over_x(half):
            v = csum[home, k, half].astype(F32)
            for slot in (1, 2, 3):
                v = v + xrecv[slot, k, half].astype(F32)
            return v

        zlsend[k] = over_x(1 - zl).astype(BF16)
        last[k] = push(zlsend.at[k], zlrecv.at[k], pair)
        fin[k] = over_x(zl)

    def do_close(k):
        last[k].wait_recv()
        mixed[k * RC:(k + 1) * RC] = (fin[k] + zlrecv[k].astype(F32)).astype(BF16)

    def do_attend(k):
        parts[k] = attend(k)

    steps = {
        "s": do_send, "f": do_forward, "r": do_route, "t": do_settle,
        "o": lambda k: pass_on(k, kz[k], kx[k]), "p": lambda k: pass_far(k, kz[k], kx[k]),
        "m": do_multiply, "F": send_far, "N": send_near, "Z": do_z, "a": lambda _: angles(),
        "q": do_squares, "E": do_fresh, "G": do_fresh_over, "Q": send_queries, "P": do_patch,
        "A": do_attend, "M": lambda k: gather_start(k, parts[k]),
        "H": lambda k: gather_z(k, (3, 1)), "I": lambda k: gather_z(k, (2,)), "K": gather_far,
        "B": do_masks, "R": do_product, "X": do_x, "D": do_pair, "C": do_close,
    }
    for step in ORDER:
        steps[step[0]](*[int(n) for n in step[1:]])
    for r in range(4):
        @pl.when(away(r) != 0)
        def _():
            for k in range(3):
                x_copy(r, k, 1).wait_send()
    for c in sent:
        c.wait_send()
    assert ids[0] <= XBASE


VM = pl.BlockSpec(memory_space=pltpu.VMEM)
SM = pl.BlockSpec(memory_space=pltpu.SMEM)
HBM = pl.BlockSpec(memory_space=pltpu.HBM)
FREQ = (THETA ** (-2.0 * (np.arange(HD) % (HD // 2)) / HD)).astype(np.float32)[None]


def shards(store, owners, positions, sel_rows, sel_hidden, norm_gain, w_query, w_keyval, w_out):
    blended, mixed = pl.pallas_call(
        sublayer,
        name="sublayer",
        out_shape=(
            jax.ShapeDtypeStruct((L, HD), BF16),
            jax.ShapeDtypeStruct((SEL, 768), BF16),
        ),
        in_specs=[SM, SM, VM, VM, VM, HBM, HBM, HBM, HBM, HBM],
        out_specs=(VM, VM),
        scratch_shapes=[
            pltpu.VMEM((16, SEL, 768), BF16),
            pltpu.VMEM((768, 768), BF16),
            pltpu.VMEM((768, HD), BF16),
            pltpu.VMEM((768, 768), BF16),
            *[pltpu.VMEM((4, 4, n, HD), BF16) for _, n in PARTS],
            pltpu.VMEM((4, L, HD), BF16),
            pltpu.VMEM((4, L, HD), BF16),
            pltpu.VMEM((1, 4, SEL, PW), BF16),
            pltpu.VMEM((2, 2, SEL, PW), BF16),
            pltpu.VMEM((3, 4, SEL, PW), F32),
            pltpu.VMEM((2, 4, SEL, PW), BF16),
            pltpu.VMEM((2, 4, SEL, PW), BF16),
            pltpu.VMEM((4, SEL, PW), BF16),
            pltpu.VMEM((4, SEL, PW), BF16),
            pltpu.VMEM((4, 8, 128), F32),
            pltpu.VMEM((4, 8, 128), F32),
            pltpu.VMEM((8, 128), F32),
            pltpu.VMEM((4, 8, 128), F32),
            pltpu.VMEM((SEL, HD), F32),
            pltpu.VMEM((2, SEL + 8, HD), F32),
            pltpu.VMEM((2, 4, L, HD), BF16),
            pltpu.VMEM((2, 4, SEL, HD), BF16),
            pltpu.VMEM((4, L, SEL), BF16),
            pltpu.VMEM((4, L, HD), F32),
            pltpu.VMEM((3, 8, TQ), F32),
            pltpu.VMEM((4, L, HD), BF16),
            pltpu.VMEM((HD, 4 * L), BF16),
            pltpu.VMEM((2, L, HD), BF16),
            pltpu.VMEM((3, TQ, HD), BF16),
            pltpu.VMEM((4, L, TQ), F32),
            pltpu.VMEM((4, L, TQ), BF16),
            pltpu.VMEM((3, TQ, HD), BF16),
            pltpu.VMEM((3, 4, 8, 256), F32),
            pltpu.VMEM((3, 4, QC, HD), BF16),
            pltpu.VMEM((3, 4, 8, 256), F32),
            pltpu.VMEM((4, 4, SEL, 768), BF16),
            pltpu.VMEM((4, 3, 2, 2, RC, 768), BF16),
            pltpu.VMEM((4, 3, 2, RC, 768), BF16),
            pltpu.VMEM((4, 3, 2, RC, 768), BF16),
            pltpu.VMEM((4, 3, 2, RC, 768), BF16),
            pltpu.VMEM((3, RC, 768), BF16),
            pltpu.VMEM((3, RC, 768), BF16),
            pltpu.VMEM((3, RC, 768), F32),
            pltpu.SemaphoreType.DMA((SEMS,)),
            pltpu.SemaphoreType.DMA((SEMS,)),
            pltpu.SemaphoreType.DMA((4 + NP,)),
        ],
        compiler_params=pltpu.CompilerParams(
            collective_id=0, has_side_effects=True, vmem_limit_bytes=60 * 2**20),
    )(owners, positions, sel_rows, norm_gain, jnp.asarray(FREQ),
      sel_hidden, w_query, w_keyval, store, w_out)
    return blended[None], mixed[None]


def solution(mesh):
    return jax.shard_map(
        shards,
        mesh=mesh,
        in_specs=(
            P("section", None, "tensor"),
            P(),
            P(),
            P(),
            P(None, None, "section"),
            P("section"),
            P("section", "tensor"),
            P("section", "tensor"),
            P("tensor", "section"),
        ),
        out_specs=(P("section", None, "tensor"), P("tensor", None, "section")),
        check_vma=False,
    )
```
